512 devices in a mesh: ctx: 16 (over y, x), exp: 32 (over z, core).
Axes of the slice: x: 4, y: 4, z: 16, core: 2. Of those that a mesh axis runs over, the one named last changes fastest.
Arguments:
- mixed_qkv: bfloat16 [32, 2048, 3072], P('exp', 'ctx'), may hold values from -6 to 6
- conv_weight: bfloat16 [4, 3072], replicated, may hold values from -2.5 to 2.5
- log_gate: float32 [32, 2048, 8], P('exp', 'ctx'), may hold values from -1 to 0
- beta: float32 [32, 2048, 8], P('exp', 'ctx'), may hold values from 0.005 to 0.05
- gate_z: bfloat16 [32, 2048, 1024], P('exp', 'ctx'), may hold values from -6 to 6
- norm_gain: float32 [128], replicated, may hold values from 0.1 to 1.9
- out_weight: bfloat16 [1024, 2048], P('exp', 'ctx'), may hold values from -0.1875 to 0.1875
- residual: bfloat16 [32, 2048, 2048], P('exp', 'ctx'), may hold values from -6 to 6
- post_gain: float32 [2048], replicated, may hold values from 0.1 to 1.9
- expert_ids: int32 [32, 2048, 1], P('exp', 'ctx'), may hold values from 0 to 31; in each aligned block of 128 rows (0 to 127, 128 to 255, ..., all dimensions but the last counted through in order) at most 8 rows name the same one
- route_weight: float32 [32, 2048, 1], P('exp', 'ctx'), may hold values from 0.2 to 1
- w_gate: bfloat16 [32, 2048, 512], P('exp', 'ctx'), may hold values from -0.125 to 0.125
- w_up: bfloat16 [32, 2048, 512], P('exp', 'ctx'), may hold values from -0.125 to 0.125
- w_down: bfloat16 [32, 512, 2048], P('exp', None, 'ctx'), may hold values from -0.25 to 0.25
Outputs:
- mixed: bfloat16 [32, 2048, 2048], P('exp', 'ctx')
The draws below stay inside these ranges and needn't reach their ends.
Inputs may be any that keep to these rules, and one draw needn't show every extreme that they name: `expert_ids`: among the rows of one device, at most 8 picks name the same expert, a bound that some block reaches.
All inputs are finite; a program needn't handle non-finite values.
Results may differ from the reference program's by a relative error of at most 0.0057.
Values may be sent and summed in bfloat16 or wider, within the bound.
A program may use at most 128 MiB of HBM per device.

```python
import math
import jax
import jax.numpy as jnp
import numpy as np
from jax import lax

D = 2048
H = 8
HD = 128
FF = 512
KW = 4
PICKS = 1
TOK_DEV = 128
SEQS = 32
LEN = 2048
EXPERTS = 32
CAP = 8
N_CTX = 16
N_EXP = 32


def draw_log_gate(key, part):
    key = jax.random.fold_in(key, 11)
    streams = jax.random.split(key, 7)
    order = jax.random.permutation(streams[0], H)
    fast_count = max(1, 3 * H // 8)
    fast = order < fast_count
    slow_rate = jax.random.uniform(streams[1], (H,), jnp.float32, 0.1, 0.3) / LEN
    fast_rate = jax.random.uniform(streams[2], (H,), jnp.float32, 0.02, 0.033)
    rate = jnp.where(fast, fast_rate, slow_rate)
    device_blocks = LEN // TOK_DEV
    device_factor = jax.random.uniform(streams[3], (SEQS, device_blocks, 1, H), jnp.float32, 0.6, 1.4)
    device_factor = jnp.broadcast_to(device_factor, (SEQS, device_blocks, TOK_DEV, H)).reshape(SEQS, LEN, H)
    rough = jax.random.uniform(streams[4], (SEQS, LEN, H), jnp.float32, 0.5, 1.5)
    spots = jax.random.randint(streams[5], (SEQS, 2), 0, LEN)
    struck = jnp.any(jnp.arange(LEN)[None, :, None] == spots[:, None, :], axis=-1).astype(jnp.float32)
    losses = jax.random.uniform(streams[6], (SEQS, LEN, H), jnp.float32, math.log(0.5), math.log(0.8))
    return (-rate * device_factor * rough + struck[..., None] * losses).astype(jnp.float32)


def block_scale(rng, dims, cuts, low, top_value):
    gain, own = 1.0, jax.random.fold_in(rng, 6)
    for position, shards_of in cuts:
        heights = jnp.exp(jax.random.uniform(jax.random.fold_in(own, position), (shards_of,), jnp.float32, low / len(cuts), top_value / len(cuts)))
        gain = gain * jnp.repeat(heights, dims[position] // shards_of).reshape([-1 if axis == position else 1 for axis in range(len(dims))])
    return gain


def routed_block(key, own, number, rows, amount, top, limit, lean):
    ranking = jax.random.permutation(key, amount)
    packed, usual = portions_of(amount, rows * top, limit, lean, True), portions_of(amount, rows * top, limit, lean, False)
    places = jnp.arange(amount)

    def named(sizes, rotation):
        used = int((sizes > 0).sum())
        fixed = max(1, used // 4)
        moved = fixed + (places - fixed + rotation * (used - fixed)) % max(1, amount - fixed)
        return jnp.zeros((amount,), jnp.int32).at[ranking[jnp.where(places < fixed, places, moved)]].set(jnp.asarray(sizes, jnp.int32))

    sizes = jnp.where(number % 4 == 0, named(packed, number // 4), named(usual, number - number // 4 - 1))
    mixed = jax.random.permutation(jax.random.fold_in(own, 3), amount)
    source_of, taker = mixed[0:amount // 2 * 2:2], mixed[1:amount // 2 * 2:2]
    slack = jnp.minimum(sizes[source_of] - 1, limit - sizes[taker]) // 2
    slack = jnp.where((source_of == ranking[0]) | (taker == ranking[0]) | (sizes[taker] == 0), 0, jnp.maximum(slack, 0))
    moved = jax.random.randint(jax.random.fold_in(own, 4), (amount // 2,), 0, 1 << 20) % (slack + 1)
    sizes = sizes.at[source_of].add(-moved).at[taker].add(moved)
    labels = jnp.searchsorted(jnp.cumsum(sizes), jnp.arange(rows * top), side="right").astype(jnp.int32)
    grid = labels.reshape(top, rows).T
    grid = grid[jax.random.permutation(jax.random.fold_in(own, 1), rows)]
    rotation = jax.random.randint(jax.random.fold_in(own, 2), (rows, 1), 0, top)
    return jnp.take_along_axis(grid, (jnp.arange(top)[None, :] + rotation) % top, axis=1)


def portions_of(amount, total, reach, lean, full):
    loads = [(1 << 20) // math.isqrt(rank ** lean) + 1 for rank in range(1, amount + 1)]
    largest = reach if full else min(reach, max(-(-total // amount), total * loads[0] // sum(loads)))
    least = 1 if total - largest >= amount - 1 else 0
    counts, surplus = [largest] + [least] * (amount - 1), total - largest - least * (amount - 1)
    while surplus > 0:
        movable = [i for i in range(1, amount) if counts[i] < largest] or [i for i in range(1, amount) if counts[i] < reach]
        whole, remaining = sum([loads[i] for i in movable]), surplus
        for i in movable:
            more = min(reach - counts[i], max(1, remaining * loads[i] // whole), surplus)
            counts[i] = counts[i] + more
            surplus = surplus - more
    return np.array(counts)


def noise(rng, extent, spread, limit, pieces=(), kind=jnp.bfloat16):
    entries = jax.random.normal(rng, extent, jnp.float32) * spread
    if len(pieces) > 0:
        entries = block_scale(rng, extent, pieces, -0.22, 0.18) * entries
    return jnp.clip(entries, min=-limit, max=limit).astype(kind)


def setup_inputs(seed: int = 0) -> dict:
    arg_keys = jax.random.split(jax.random.key(seed), 15)
    mixed_qkv = noise(arg_keys[0], (SEQS, LEN, 3 * H * HD), 1.0, 6.0, ((0, 32), (1, 16)))
    conv_weight = noise(arg_keys[1], (KW, 3 * H * HD), 0.5, 2.5)
    log_gate = draw_log_gate(jax.random.fold_in(arg_keys[14], 71), 0)
    beta = jnp.clip(jnp.exp(math.log(0.05) - 2.3025851 * jax.random.uniform(arg_keys[3], (SEQS, LEN, H), jnp.float32) ** block_scale(arg_keys[3], (SEQS, LEN, H), ((0, 32), (1, 16)), -0.2, 0.2)), 0.005, 0.05)
    gate_z = noise(arg_keys[4], (SEQS, LEN, H * HD), 1.0, 6.0, ((0, 32), (1, 16)))
    norm_gain = jnp.clip(1.0 + 0.18 * jax.random.normal(arg_keys[5], (HD,), jnp.float32), 0.1, 1.9)
    out_weight = noise(arg_keys[6], (H * HD, D), (H * HD) ** -0.5, 0.1875, ((0, 32), (1, 16)))
    residual = noise(arg_keys[7], (SEQS, LEN, D), 1.0, 6.0, ((0, 32), (1, 16)))
    post_gain = jnp.clip(1.0 + 0.18 * jax.random.normal(arg_keys[8], (D,), jnp.float32), 0.1, 1.9)
    expert_ids_keys = jax.random.split(jax.random.fold_in(arg_keys[9], 1), SEQS * LEN // TOK_DEV)
    expert_ids_turns = jax.random.permutation(jax.random.fold_in(arg_keys[9], 3), SEQS * LEN // TOK_DEV)
    expert_ids = jax.vmap(lambda own, number: routed_block(jax.random.fold_in(arg_keys[9], 2), own, number, TOK_DEV, EXPERTS, PICKS, CAP, 2))(expert_ids_keys, expert_ids_turns).reshape((SEQS, LEN, PICKS))
    route_weight = jnp.clip(0.2 + 0.8 * jax.random.uniform(arg_keys[10], (SEQS, LEN, PICKS), jnp.float32) ** block_scale(arg_keys[10], (SEQS, LEN, PICKS), ((0, 32), (1, 16)), -0.2, 0.2), 0.2, 1.0)
    w_gate = noise(arg_keys[11], (EXPERTS, D, FF), D ** -0.5, 0.125, ((0, 32), (1, 16)))
    w_up = noise(arg_keys[12], (EXPERTS, D, FF), D ** -0.5, 0.125, ((0, 32), (1, 16)))
    w_down = noise(arg_keys[13], (EXPERTS, FF, D), FF ** -0.5, 0.25, ((0, 32), (2, 16)))
    return {"mixed_qkv": mixed_qkv, "conv_weight": conv_weight, "log_gate": log_gate, "beta": beta, "gate_z": gate_z, "norm_gain": norm_gain, "out_weight": out_weight, "residual": residual, "post_gain": post_gain, "expert_ids": expert_ids, "route_weight": route_weight, "w_gate": w_gate, "w_up": w_up, "w_down": w_down}


exact_mode = lax.Precision.HIGHEST
norm_eps = 1e-06

def unit_rows(rows):
    return rows * lax.rsqrt(lax.optimization_barrier(jnp.sum(rows * rows, axis=-1, keepdims=True)) + norm_eps)

def reference(mixed_qkv, conv_weight, log_gate, beta, gate_z, norm_gain, out_weight, residual, post_gain, expert_ids, route_weight, w_gate, w_up, w_down):
    seqs, length, width = mixed_qkv.shape
    heads = log_gate.shape[2]
    head_dim = width // (3 * heads)
    inner = heads * head_dim
    model_dim = residual.shape[2]
    picks = expert_ids.shape[2]
    taps = conv_weight.shape[0]
    padded = jnp.pad(mixed_qkv.astype(jnp.float32), ((0, 0), (taps - 1, 0), (0, 0)))
    filters = conv_weight.astype(jnp.float32)
    filtered = padded[:, 0:length] * filters[0]
    for offset in range(1, taps):
        filtered = filtered + padded[:, offset:offset + length] * filters[offset]
    active = jax.nn.silu(filtered)
    queries = unit_rows(active[..., :inner].reshape(seqs, length, heads, head_dim)) * head_dim ** (-0.5)
    keys = unit_rows(active[..., inner:2 * inner].reshape(seqs, length, heads, head_dim))
    values = active[..., 2 * inner:].reshape(seqs, length, heads, head_dim)

    def advance(state, member):
        query_now, key_now, value_now, gate_now, strength = member
        recalled = jnp.einsum('shd,shde->she', key_now, state, precision=exact_mode)
        state = jnp.exp(gate_now)[..., None, None] * (state - strength[..., None, None] * key_now[..., :, None] * recalled[..., None, :]) + strength[..., None, None] * key_now[..., :, None] * value_now[..., None, :]
        return (state, jnp.einsum('shd,shde->she', query_now, state, precision=exact_mode))
    series = tuple((jnp.moveaxis(array, 1, 0) for array in (queries, keys, values, log_gate, beta)))
    initial = jnp.zeros((seqs, heads, head_dim, head_dim), jnp.float32)
    unused, core = lax.scan(advance, initial, series)
    core = jnp.moveaxis(core, 0, 1)
    gates = gate_z.astype(jnp.float32).reshape(seqs, length, heads, head_dim)
    scale_rms = lax.rsqrt(lax.optimization_barrier(jnp.mean(core * core, axis=-1, keepdims=True)) + norm_eps)
    normed = (core * scale_rms * norm_gain * jax.nn.silu(gates)).reshape(seqs * length, inner).astype(jnp.bfloat16)
    attended = jnp.dot(normed, out_weight, preferred_element_type=jnp.float32)
    hidden = (residual.reshape(seqs * length, model_dim).astype(jnp.float32) + attended).astype(jnp.bfloat16)
    stream = lax.optimization_barrier(hidden).astype(jnp.float32)
    routed_in = (stream * lax.rsqrt(lax.optimization_barrier(jnp.mean(stream * stream, axis=-1, keepdims=True)) + norm_eps) * post_gain).astype(jnp.bfloat16)
    total_rows = seqs * length * picks
    routed = expert_ids.reshape(total_rows)
    repeated = jnp.broadcast_to(routed_in[:, None, :], (seqs * length, picks, model_dim)).reshape(total_rows, model_dim)
    most_rows = CAP * N_CTX * N_EXP

    def serve_expert(result, member):
        index, gate_w, up_w, down_w = member
        picked = jnp.nonzero(routed == index, size=most_rows, fill_value=total_rows)[0].astype(jnp.int32)
        rows_in = repeated[jnp.minimum(picked, total_rows - 1)].astype(jnp.float32)
        gate_part = jnp.dot(rows_in, gate_w.astype(jnp.float32))
        up_part = jnp.dot(rows_in, up_w.astype(jnp.float32))
        activated = (jax.nn.silu(gate_part) * up_part).astype(jnp.bfloat16)
        answer = jnp.dot(activated.astype(jnp.float32), down_w.astype(jnp.float32)).astype(jnp.bfloat16)
        return (result.at[picked].set(answer, mode='drop'), None)
    blank = jnp.zeros((total_rows, model_dim), jnp.bfloat16)
    indices = jnp.arange(w_gate.shape[0], dtype=jnp.int32)
    fetched, unused = lax.scan(serve_expert, blank, (indices, w_gate, w_up, w_down))
    fetched = fetched.astype(jnp.float32).reshape(seqs * length, picks, model_dim)
    weights = route_weight.reshape(seqs * length, picks)
    mixed = stream + lax.optimization_barrier(jnp.sum(weights[..., None] * fetched, axis=1))
    return mixed.astype(jnp.bfloat16).reshape(seqs, length, model_dim)
```

```python
import functools
import math

import jax
import jax.numpy as jnp
from jax import lax
from jax.experimental import pallas as pl
from jax.experimental.pallas import tpu as pltpu
from jax.sharding import PartitionSpec as P

MESH = pl.DeviceIdType.MESH
F32, BF16 = jnp.float32, jnp.bfloat16
NN, NT, TN = ((1,), (0,)), ((1,), (1,)), ((0,), (0,))
EPS = 1e-06
HD = 128
HALO = 16


def dot(a, b, dims=NN):
    return lax.dot_general(
        a.astype(BF16), b.astype(BF16), (dims, ((), ())), preferred_element_type=F32
    )


def silu(u):
    return u / (1.0 + jnp.exp(-u))


def copy_to(src, dst, send, recv, **where):
    return pltpu.make_async_remote_copy(
        src_ref=src,
        dst_ref=dst,
        send_sem=send,
        recv_sem=recv,
        device_id=where,
        device_id_type=MESH,
    )


def loop(low, high, body):
    lax.fori_loop(low, high, lambda i, c: (body(i), c)[1], 0)


def kernel(
    n_ctx,
    n_exp,
    side,
    qkv_ref,
    taps_ref,
    lgate_ref,
    beta_ref,
    z_ref,
    gain_ref,
    ow_ref,
    res_ref,
    post_ref,
    ids_ref,
    rw_ref,
    wg_ref,
    wu_ref,
    wd_ref,
    out_ref,
    halo,
    xs,
    keys,
    queries,
    decays,
    solved,
    ab_send,
    ab_recv,
    st_send,
    st_recv,
    qmap,
    lout,
    normed,
    colblk,
    wbuf,
    hidden,
    gate_full,
    up_full,
    down_full,
    outbound,
    arrived,
    answer,
    returned,
    halo_s,
    halo_r,
    col_s,
    col_r,
    band_s,
    band_r,
    core_s,
    core_r,
    ab_s,
    ab_r,
    st_s,
    st_r,
    w1_s,
    w1_r,
    w2_s,
    w2_r,
    out_s,
    out_r,
    back_s,
    back_r,
):
    ctx, exp = lax.axis_index("ctx"), lax.axis_index("exp")
    row, col = ctx // side, ctx % side
    tokens, width = qkv_ref.shape
    heads = width // (3 * HD)
    inner = heads * HD
    model = res_ref.shape[1]
    halfm = model // 2
    lanes = ow_ref.shape[1]
    slab = ow_ref.shape[0]
    cap = outbound.shape[1] // 2
    wrows = wg_ref.shape[0]
    sibling = exp + 1 - 2 * (exp % 2)
    half_in = inner // 2
    mine = pl.ds(pl.multiple_of((exp % 2) * half_in, half_in), half_in)
    theirs = pl.ds(pl.multiple_of((1 - exp % 2) * half_in, half_in), half_in)

    barrier = pltpu.get_barrier_semaphore()

    def greet_ctx(d):
        pl.semaphore_signal(
            barrier, inc=1, device_id={"ctx": (ctx + d) % n_ctx}, device_id_type=MESH
        )

    def greet_exp(d):
        pl.semaphore_signal(
            barrier, inc=1, device_id={"exp": (exp + d) % n_exp}, device_id_type=MESH
        )

    loop(1, n_ctx, greet_ctx)
    loop(1, n_exp, greet_exp)
    pl.semaphore_wait(barrier, n_ctx + n_exp - 2)

    halo_copy = copy_to(
        qkv_ref.at[pl.ds(tokens - HALO, HALO), :],
        halo,
        halo_s.at[0],
        halo_r.at[0],
        ctx=(ctx + 1) % n_ctx,
    )
    halo_copy.start()
    my_slab = pl.ds(pl.multiple_of(exp * slab, slab), slab)

    def col_copy(d):
        return copy_to(
            ow_ref, colblk.at[my_slab, :], col_s.at[d], col_r.at[d], exp=(exp + d) % n_exp
        )

    loop(1, n_exp, lambda d: col_copy(d).start())
    colblk[my_slab, :] = ow_ref[...]

    def along_x(d):
        return row * side + (col + d) % side

    def along_y(d):
        return ((row + d) % side) * side + col

    def w1_copies(d):
        return (
            copy_to(wg_ref, gate_full.at[row, col], w1_s.at[0, d], w1_r.at[0, d], ctx=along_x(d)),
            copy_to(wu_ref, up_full.at[row, col], w1_s.at[1, d], w1_r.at[1, d], ctx=along_y(d)),
            copy_to(
                wd_ref.at[pl.ds(0, wd_ref.shape[0] // 2), :],
                down_full.at[0, row, col],
                w1_s.at[2, d],
                w1_r.at[2, d],
                ctx=along_x(d),
            ),
            copy_to(
                wd_ref.at[pl.ds(wd_ref.shape[0] // 2, wd_ref.shape[0] // 2), :],
                down_full.at[1, row, col],
                w1_s.at[3, d],
                w1_r.at[3, d],
                ctx=along_y(d),
            ),
        )

    def w2_copies(d):
        return (
            copy_to(
                gate_full.at[row], gate_full.at[row], w2_s.at[0, d], w2_r.at[0, d], ctx=along_y(d)
            ),
            copy_to(
                up_full.at[:, col], up_full.at[:, col], w2_s.at[1, d], w2_r.at[1, d], ctx=along_x(d)
            ),
            copy_to(
                down_full.at[0, row],
                down_full.at[0, row],
                w2_s.at[2, d],
                w2_r.at[2, d],
                ctx=along_y(d),
            ),
            copy_to(
                down_full.at[1, :, col],
                down_full.at[1, :, col],
                w2_s.at[3, d],
                w2_r.at[3, d],
                ctx=along_x(d),
            ),
        )

    for d in range(1, side):
        for c in w1_copies(d):
            c.start()
    gate_full[row, col] = wg_ref[...]
    up_full[row, col] = wu_ref[...]
    down_full[0, row, col] = wd_ref[: wd_ref.shape[0] // 2, :]
    down_full[1, row, col] = wd_ref[wd_ref.shape[0] // 2 :, :]

    xs[8:, :] = qkv_ref[...].astype(F32)
    tri_r = lax.broadcasted_iota(jnp.int32, (tokens, tokens), 0)
    tri_c = lax.broadcasted_iota(jnp.int32, (tokens, tokens), 1)
    causal = tri_r >= tri_c
    strict = tri_r > tri_c
    eye = (tri_r == tri_c).astype(F32)
    growth_col = lax.dot_general(
        causal.astype(F32),
        lgate_ref[...],
        (NN, ((), ())),
        preferred_element_type=F32,
        precision=lax.Precision.HIGHEST,
    )
    last = growth_col[tokens - 1 :, :]
    strength = beta_ref[...]
    halo_copy.wait()
    xs[:8, :] = jnp.where(ctx > 0, halo[...].astype(F32)[HALO - 8 :, :], 0.0)
    taps = taps_ref[...].astype(F32)

    def active(block):
        at = slice(block * HD, (block + 1) * HD)
        total = xs[5 : 5 + tokens, at] * taps[0:1, at]
        for j in range(1, 4):
            total = total + xs[5 + j : 5 + j + tokens, at] * taps[j : j + 1, at]
        return silu(total)

    def unit(rows):
        return rows * lax.rsqrt(jnp.sum(rows * rows, axis=-1, keepdims=True) + EPS)

    lowers = []
    for h in range(heads):
        q = unit(active(h)) * HD ** (-0.5)
        k = unit(active(heads + h))
        queries[h] = q
        keys[h] = k
        gc = growth_col[:, h : h + 1]
        gr = jnp.sum(gc * eye, axis=0, keepdims=True)
        decay = jnp.where(causal, jnp.exp(jnp.where(causal, gc - gr, 0.0)), 0.0)
        decays[h] = decay
        kk = dot(k, k, NT)
        lowers.append(jnp.where(strict, strength[:, h : h + 1] * decay * kk, 0.0))

    def same(size):
        return tri_r // size == tri_c // size

    base = 16
    near = same(base)
    power = [jnp.where(near, l, 0.0) for l in lowers]
    inv = [eye - p for p in power]
    for _ in range(3):
        power = [dot(p, p) for p in power]
        inv = [x + dot(x, p) for x, p in zip(inv, power)]
    size = base
    while size < tokens:
        ring = jnp.logical_and(same(2 * size), jnp.logical_not(same(size)))
        mid = [dot(jnp.where(ring, l, 0.0), x) for l, x in zip(lowers, inv)]
        inv = [x - dot(x, m) for x, m in zip(inv, mid)]
        size *= 2

    def col_wait(d):
        c = col_copy(d)
        c.wait_send()
        c.wait_recv()

    loop(1, n_exp, col_wait)

    def band_copy(d):
        return copy_to(
            colblk.at[mine, :],
            wbuf.at[ctx, mine, :],
            band_s.at[d],
            band_r.at[d],
            ctx=(ctx + d) % n_ctx,
        )

    loop(1, n_ctx, lambda d: band_copy(d).start())
    wbuf[ctx] = colblk[...]

    for h in range(heads):
        b = strength[:, h : h + 1]
        gc = growth_col[:, h : h + 1]
        k = keys[h]
        v = active(2 * heads + h)
        rhs = jnp.concatenate([(b * jnp.exp(gc)) * k, b * v], axis=1)
        sol = dot(inv[h], rhs).astype(BF16)
        solved[h] = sol
        kept = jnp.exp(last[:, h : h + 1] - gc) * k
        both = dot(sol, kept, TN)
        at = (jnp.exp(last[:, h : h + 1]) * eye - both[:HD, :]).astype(BF16)
        bt = both[HD:, :].astype(BF16)
        ab_send[2 * h, :HD, :] = at
        ab_send[2 * h + 1, :HD, :] = at
        ab_send[2 * h, HD:, :] = bt[: HD // 2, :]
        ab_send[2 * h + 1, HD:, :] = bt[HD // 2 :, :]

    def ab_copy(d):
        to = (ctx + d) % n_ctx
        return copy_to(ab_send.at[to], ab_recv.at[ctx], ab_s.at[d], ab_r.at[d], ctx=to)

    loop(1, n_ctx, lambda d: ab_copy(d).start())
    ab_recv[ctx] = ab_send[ctx]

    for h in range(heads):
        gc = growth_col[:, h : h + 1]
        q = queries[h]
        qk = decays[h] * dot(q, keys[h], NT)
        both = dot(qk, solved[h])
        qmap[h] = (jnp.exp(gc) * q - both[:, :HD]).astype(BF16)
        lout[h] = both[:, HD:]

    def ab_wait(d):
        c = ab_copy(d)
        c.wait_send()
        c.wait_recv()

    loop(1, n_ctx, ab_wait)
    half = HD // 2
    state = jnp.zeros((half, HD), F32)
    for c in range(n_ctx):
        high = state.astype(BF16)
        st_send[c] = high
        if c < n_ctx - 1:
            low = (state - high.astype(F32)).astype(BF16)
            parts = dot(jnp.concatenate([high, low], axis=0), ab_recv[c, :HD, :])
            state = parts[:half] + parts[half:] + ab_recv[c, HD:, :].astype(F32)

    def st_copy(d):
        to = (ctx + d) % n_ctx
        return copy_to(st_send.at[to], st_recv.at[ctx], st_s.at[d], st_r.at[d], ctx=to)

    loop(1, n_ctx, lambda d: st_copy(d).start())
    st_recv[ctx] = st_send[ctx]

    def core_copy(d):
        src = (ctx + n_ctx - d) % n_ctx
        return copy_to(
            wbuf.at[src, mine, :],
            wbuf.at[src, mine, :],
            core_s.at[d],
            core_r.at[d],
            exp=sibling,
        )

    def forward(d):
        c = band_copy(d)
        c.wait_send()
        c.wait_recv()
        core_copy(d).start()

    loop(1, n_ctx, forward)

    def st_wait(d):
        c = st_copy(d)
        c.wait_send()
        c.wait_recv()

    loop(1, n_ctx, st_wait)

    for d in range(1, side):
        for c in w1_copies(d):
            c.wait_send()
            c.wait_recv()
    for d in range(1, side):
        for c in w2_copies(d):
            c.start()

    gain = gain_ref[...]
    for h in range(heads):
        st = jnp.concatenate([st_recv[2 * h], st_recv[2 * h + 1]], axis=0)
        core = dot(qmap[h], st, NT) + lout[h]
        scale = lax.rsqrt(jnp.mean(core * core, axis=-1, keepdims=True) + EPS)
        z = z_ref[:, h * HD : (h + 1) * HD].astype(F32)
        normed[:, h * HD : (h + 1) * HD] = (core * scale * gain * silu(z)).astype(BF16)

    def core_wait(d):
        c = core_copy(d)
        c.wait_send()
        c.wait_recv()

    loop(1, n_ctx, core_wait)

    squares = jnp.zeros((tokens, 1), F32)
    act = normed[...]
    for j in range(n_ctx):
        at = slice(j * lanes, (j + 1) * lanes)
        hid = (res_ref[:, at].astype(F32) + dot(act, wbuf[j])).astype(BF16)
        hidden[:, at] = hid
        hid = hid.astype(F32)
        squares = squares + jnp.sum(hid * hid, axis=-1, keepdims=True)
    scale = lax.rsqrt(squares / model + EPS)
    routed_in = (hidden[...].astype(F32) * scale * post_ref[...]).astype(BF16)

    ids = ids_ref[...]
    member = lax.broadcasted_iota(jnp.int32, (tokens, n_exp), 1) == ids
    member = member.astype(F32)
    ranks = dot(causal.astype(F32), member)
    slot = jnp.sum(ranks * member, axis=1, keepdims=True).astype(jnp.int32) - 1
    first = ids * (2 * cap) + slot
    places = lax.broadcasted_iota(jnp.int32, (tokens, 2 * cap * n_exp), 1)
    pick_low = (places == first).astype(F32).astype(BF16)
    pick_high = (places == first + cap).astype(F32).astype(BF16)
    sent = dot(pick_low, routed_in[:, :halfm], TN) + dot(pick_high, routed_in[:, halfm:], TN)
    outbound[...] = sent.astype(BF16).reshape(outbound.shape)

    def out_copy(d):
        to = (exp + d) % n_exp
        return copy_to(outbound.at[to], arrived.at[exp], out_s.at[d], out_r.at[d], exp=to)

    loop(1, n_exp, lambda d: out_copy(d).start())
    arrived[exp] = outbound[exp]

    for d in range(1, side):
        for c in w2_copies(d):
            c.wait_send()
            c.wait_recv()

    def out_wait(d):
        c = out_copy(d)
        c.wait_send()
        c.wait_recv()

    loop(1, n_exp, out_wait)

    ff = wg_ref.shape[1]
    came = arrived[...].astype(F32)
    rows_in = jnp.concatenate(
        [
            came[:, :cap, :].reshape(n_exp * cap, halfm),
            came[:, cap:, :].reshape(n_exp * cap, halfm),
        ],
        axis=1,
    ).astype(BF16)
    gate_part = dot(rows_in, gate_full[...].reshape(model, ff))
    up_part = dot(rows_in, up_full[...].reshape(model, ff))
    activated = (silu(gate_part) * up_part).astype(BF16)
    blocks = n_ctx // 2
    for j in range(blocks):
        parts = []
        for i in (j, j + blocks):
            down = jnp.concatenate(
                [down_full[0, i // side, i % side], down_full[1, i // side, i % side]], axis=0
            )
            parts.append(dot(activated, down).reshape(n_exp, cap, lanes))
        answer[:, :, j * lanes : (j + 1) * lanes] = jnp.concatenate(parts, axis=1).astype(BF16)

    def back_copy(d):
        to = (exp + d) % n_exp
        return copy_to(answer.at[to], returned.at[exp], back_s.at[d], back_r.at[d], exp=to)

    loop(1, n_exp, lambda d: back_copy(d).start())
    returned[exp] = answer[exp]

    def back_wait(d):
        c = back_copy(d)
        c.wait_send()
        c.wait_recv()

    loop(1, n_exp, back_wait)

    back = returned[...].reshape(2 * cap * n_exp, halfm)
    weight = rw_ref[...]
    for pick, at in ((pick_low, slice(0, halfm)), (pick_high, slice(halfm, model))):
        fetched = dot(pick, back)
        out_ref[:, at] = (hidden[:, at].astype(F32) + weight * fetched).astype(BF16)


def on_device(n_ctx, n_exp, *args):
    (qkv, taps, lgate, beta, z, gain, ow, res, post, ids, rw, wg, wu, wd) = args
    tokens, width = qkv.shape[1:]
    heads = lgate.shape[2]
    model = res.shape[2]
    ff = wg.shape[2]
    side = math.isqrt(n_ctx)
    cap = 2 * ids.shape[2] * tokens // n_exp
    inner = heads * HD
    lanes = ow.shape[1]
    sem = pltpu.SemaphoreType.DMA
    slots = (n_exp, 2 * cap, model // 2)
    scratch = [
        pltpu.VMEM((HALO, width), BF16),
        pltpu.VMEM((8 + tokens, width), F32),
        pltpu.VMEM((heads, tokens, HD), F32),
        pltpu.VMEM((heads, tokens, HD), F32),
        pltpu.VMEM((heads, tokens, tokens), F32),
        pltpu.VMEM((heads, tokens, 2 * HD), BF16),
        pltpu.VMEM((n_ctx, HD + HD // 2, HD), BF16),
        pltpu.VMEM((n_ctx, HD + HD // 2, HD), BF16),
        pltpu.VMEM((n_ctx, HD // 2, HD), BF16),
        pltpu.VMEM((n_ctx, HD // 2, HD), BF16),
        pltpu.VMEM((heads, tokens, HD), BF16),
        pltpu.VMEM((heads, tokens, HD), F32),
        pltpu.VMEM((tokens, inner), BF16),
        pltpu.VMEM((inner, lanes), BF16),
        pltpu.VMEM((n_ctx, inner, lanes), BF16),
        pltpu.VMEM((tokens, model), BF16),
        pltpu.VMEM((side, side, model // n_ctx, ff), BF16),
        pltpu.VMEM((side, side, model // n_ctx, ff), BF16),
        pltpu.VMEM((2, side, side, ff // 2, lanes), BF16),
        pltpu.VMEM(slots, BF16),
        pltpu.VMEM(slots, BF16),
        pltpu.VMEM(slots, BF16),
        pltpu.VMEM(slots, BF16),
        sem((1,)),
        sem((1,)),
        sem((n_exp,)),
        sem((n_exp,)),
        sem((n_ctx,)),
        sem((n_ctx,)),
        sem((n_ctx,)),
        sem((n_ctx,)),
        sem((n_ctx,)),
        sem((n_ctx,)),
        sem((n_ctx,)),
        sem((n_ctx,)),
        sem((4, side)),
        sem((4, side)),
        sem((4, side)),
        sem((4, side)),
        sem((n_exp,)),
        sem((n_exp,)),
        sem((n_exp,)),
        sem((n_exp,)),
    ]
    out = pl.pallas_call(
        functools.partial(kernel, n_ctx, n_exp, side),
        out_shape=jax.ShapeDtypeStruct((tokens, model), BF16),
        in_specs=[pl.BlockSpec(memory_space=pltpu.VMEM)] * 14,
        out_specs=pl.BlockSpec(memory_space=pltpu.VMEM),
        scratch_shapes=scratch,
        compiler_params=pltpu.CompilerParams(
            collective_id=0, has_side_effects=True, vmem_limit_bytes=48 * 2**20
        ),
    )(
        qkv[0],
        taps,
        lgate[0],
        beta[0],
        z[0],
        gain[None],
        ow,
        res[0],
        post[None],
        ids[0],
        rw[0],
        wg[0],
        wu[0],
        wd[0],
    )
    return out[None]


def solution(mesh):
    placed = (
        P("exp", "ctx", None),
        P(),
        P("exp", "ctx", None),
        P("exp", "ctx", None),
        P("exp", "ctx", None),
        P(),
        P("exp", "ctx"),
        P("exp", "ctx", None),
        P(),
        P("exp", "ctx", None),
        P("exp", "ctx", None),
        P("exp", "ctx", None),
        P("exp", "ctx", None),
        P("exp", None, "ctx"),
    )
    return jax.shard_map(
        functools.partial(on_device, mesh.shape["ctx"], mesh.shape["exp"]),
        mesh=mesh,
        in_specs=placed,
        out_specs=P("exp", "ctx", None),
        check_vma=False,
    )
```

```python
import functools
import math

import jax
import jax.numpy as jnp
from jax import lax
from jax.experimental import pallas as pl
from jax.experimental.pallas import tpu as pltpu
from jax.sharding import PartitionSpec as P

MESH = pl.DeviceIdType.MESH
F32, BF16 = jnp.float32, jnp.bfloat16
NN, NT, TN = ((1,), (0,)), ((1,), (1,)), ((0,), (0,))
EPS = 1e-06
HD = 128
HALO = 16


def dot(a, b, dims=NN):
    return lax.dot_general(
        a.astype(BF16), b.astype(BF16), (dims, ((), ())), preferred_element_type=F32
    )


def silu(u):
    return u / (1.0 + jnp.exp(-u))


def copy_to(src, dst, send, recv, **where):
    return pltpu.make_async_remote_copy(
        src_ref=src,
        dst_ref=dst,
        send_sem=send,
        recv_sem=recv,
        device_id=where,
        device_id_type=MESH,
    )


def loop(low, high, body):
    lax.fori_loop(low, high, lambda i, c: (body(i), c)[1], 0)


def kernel(
    n_ctx,
    n_exp,
    side,
    qkv_hbm,
    taps_hbm,
    lgate_hbm,
    beta_hbm,
    z_hbm,
    gain_hbm,
    ow_hbm,
    res_hbm,
    post_hbm,
    ids_hbm,
    rw_hbm,
    wg_ref,
    wu_ref,
    wd_ref,
    out_ref,
    qkv_ref,
    taps_ref,
    lgate_ref,
    beta_ref,
    z_ref,
    gain_ref,
    ow_ref,
    res_ref,
    post_ref,
    ids_ref,
    rw_ref,
    halo,
    xs,
    keys,
    queries,
    decays,
    solved,
    ab_send,
    ab_recv,
    st_send,
    st_recv,
    qmap,
    lout,
    normed,
    colblk,
    wbuf,
    hidden,
    gate_full,
    up_full,
    down_full,
    outbound,
    arrived,
    answer,
    returned,
    load_s,
    own_s,
    halo_s,
    halo_r,
    col_s,
    col_r,
    band1_s,
    band1_r,
    band2_s,
    band2_r,
    core_s,
    core_r,
    ab_s,
    ab_r,
    st_s,
    st_r,
    w1_s,
    w1_r,
    w2_s,
    w2_r,
    out_s,
    out_r,
    back_s,
    back_r,
):
    ctx, exp = lax.axis_index("ctx"), lax.axis_index("exp")
    row, col = ctx // side, ctx % side
    tokens, width = qkv_ref.shape
    heads = width // (3 * HD)
    inner = heads * HD
    model = res_ref.shape[1]
    halfm = model // 2
    lanes = ow_ref.shape[1]
    slab = ow_ref.shape[0]
    cap = outbound.shape[1] // 2
    wrows = wg_ref.shape[0]
    chip, core = exp // 2, exp % 2
    chips = n_exp // 2
    sibling = exp + 1 - 2 * core
    composer = ctx % 2 == core

    barrier = pltpu.get_barrier_semaphore()

    def greet_ctx(d):
        pl.semaphore_signal(
            barrier, inc=1, device_id={"ctx": (ctx + d) % n_ctx}, device_id_type=MESH
        )

    def greet_exp(d):
        pl.semaphore_signal(
            barrier, inc=1, device_id={"exp": (exp + d) % n_exp}, device_id_type=MESH
        )

    loop(1, n_ctx, greet_ctx)
    loop(1, n_exp, greet_exp)
    loads = [
        pltpu.make_async_copy(src, dst, load_s.at[i])
        for i, (src, dst) in enumerate(
            (
                (qkv_hbm, qkv_ref),
                (taps_hbm, taps_ref),
                (lgate_hbm, lgate_ref),
                (beta_hbm, beta_ref),
                (ow_hbm, ow_ref),
                (z_hbm, z_ref),
                (gain_hbm, gain_ref),
                (res_hbm, res_ref),
                (post_hbm, post_ref),
                (ids_hbm, ids_ref),
                (rw_hbm, rw_ref),
            )
        )
    ]
    for c in loads:
        c.start()
    owns = [
        pltpu.make_async_copy(src, dst, own_s.at[i])
        for i, (src, dst) in enumerate(
            (
                (wg_ref, gate_full.at[row, col]),
                (wu_ref, up_full.at[row, col]),
                (wd_ref.at[pl.ds(0, wd_ref.shape[0] // 2), :], down_full.at[0, row, col]),
                (
                    wd_ref.at[pl.ds(wd_ref.shape[0] // 2, wd_ref.shape[0] // 2), :],
                    down_full.at[1, row, col],
                ),
            )
        )
    ]
    for c in owns:
        c.start()
    for c in loads[:5]:
        c.wait()
    xs[8:, :] = qkv_ref[...].astype(F32)
    pl.semaphore_wait(barrier, n_ctx + n_exp - 2)

    halo_copy = copy_to(
        qkv_ref.at[pl.ds(tokens - HALO, HALO), :],
        halo,
        halo_s.at[0],
        halo_r.at[0],
        ctx=(ctx + 1) % n_ctx,
    )
    halo_copy.start()

    def col_copy(d):
        return copy_to(
            ow_ref, colblk.at[chip], col_s.at[d], col_r.at[d], exp=(exp + 2 * d) % n_exp
        )

    loop(1, chips, lambda d: col_copy(d).start())
    colblk[chip] = ow_ref[...]

    def along_x(d):
        return row * side + (col + d) % side

    def along_y(d):
        return ((row + d) % side) * side + col

    def w1_copies(d):
        return (
            copy_to(wg_ref, gate_full.at[row, col], w1_s.at[0, d], w1_r.at[0, d], ctx=along_x(d)),
            copy_to(wu_ref, up_full.at[row, col], w1_s.at[1, d], w1_r.at[1, d], ctx=along_y(d)),
            copy_to(
                wd_ref.at[pl.ds(0, wd_ref.shape[0] // 2), :],
                down_full.at[0, row, col],
                w1_s.at[2, d],
                w1_r.at[2, d],
                ctx=along_x(d),
            ),
            copy_to(
                wd_ref.at[pl.ds(wd_ref.shape[0] // 2, wd_ref.shape[0] // 2), :],
                down_full.at[1, row, col],
                w1_s.at[3, d],
                w1_r.at[3, d],
                ctx=along_y(d),
            ),
        )

    def w2_copies(d):
        return (
            copy_to(
                gate_full.at[row], gate_full.at[row], w2_s.at[0, d], w2_r.at[0, d], ctx=along_y(d)
            ),
            copy_to(
                up_full.at[:, col], up_full.at[:, col], w2_s.at[1, d], w2_r.at[1, d], ctx=along_x(d)
            ),
            copy_to(
                down_full.at[0, row],
                down_full.at[0, row],
                w2_s.at[2, d],
                w2_r.at[2, d],
                ctx=along_y(d),
            ),
            copy_to(
                down_full.at[1, :, col],
                down_full.at[1, :, col],
                w2_s.at[3, d],
                w2_r.at[3, d],
                ctx=along_x(d),
            ),
        )

    for d in range(1, side):
        for c in w1_copies(d):
            c.start()

    tri_r = lax.broadcasted_iota(jnp.int32, (tokens, tokens), 0)
    tri_c = lax.broadcasted_iota(jnp.int32, (tokens, tokens), 1)
    causal = tri_r >= tri_c
    strict = tri_r > tri_c
    eye = (tri_r == tri_c).astype(F32)
    growth_row = lax.dot_general(
        lgate_ref[...],
        (tri_r <= tri_c).astype(F32),
        (NN, ((), ())),
        preferred_element_type=F32,
        precision=lax.Precision.HIGHEST,
    )

    def column(line):
        return jnp.sum(line * eye, axis=1, keepdims=True)

    growth = [growth_row[h : h + 1, :] for h in range(heads)]
    growth_col = [column(g) for g in growth]
    last = [g[:, tokens - 1 :] for g in growth]
    strength = [column(beta_ref[h : h + 1, :]) for h in range(heads)]
    halo_copy.wait()
    xs[:8, :] = jnp.where(ctx > 0, halo[...].astype(F32)[HALO - 8 :, :], 0.0)
    taps = taps_ref[...].astype(F32)

    def active(block):
        at = slice(block * HD, (block + 1) * HD)
        total = xs[5 : 5 + tokens, at] * taps[0:1, at]
        for j in range(1, 4):
            total = total + xs[5 + j : 5 + j + tokens, at] * taps[j : j + 1, at]
        return silu(total)

    def unit(rows):
        return rows * lax.rsqrt(jnp.sum(rows * rows, axis=-1, keepdims=True) + EPS)

    lowers = []
    for h in range(heads):
        q = unit(active(h)) * HD ** (-0.5)
        k = unit(active(heads + h))
        queries[h] = q
        keys[h] = k
        gc, gr = growth_col[h], growth[h]
        decay = jnp.where(causal, jnp.exp(jnp.where(causal, gc - gr, 0.0)), 0.0)
        decays[h] = decay
        kk = dot(k, k, NT)
        lowers.append(jnp.where(strict, strength[h] * decay * kk, 0.0))

    def same(size):
        return tri_r // size == tri_c // size

    base = 16
    near = same(base)
    power = [jnp.where(near, l, 0.0) for l in lowers]
    inv = [eye - p for p in power]
    for _ in range(3):
        power = [dot(p, p) for p in power]
        inv = [x + dot(x, p) for x, p in zip(inv, power)]
    size = base
    while size < tokens:
        ring = jnp.logical_and(same(2 * size), jnp.logical_not(same(size)))
        mid = [dot(jnp.where(ring, l, 0.0), x) for l, x in zip(lowers, inv)]
        inv = [x - dot(x, m) for x, m in zip(inv, mid)]
        size *= 2

    def col_wait(d):
        c = col_copy(d)
        c.wait_send()
        c.wait_recv()

    loop(1, chips, col_wait)
    fore, rear = pl.ds(0, chips // 2), pl.ds(chips // 2, chips // 2)

    def band1_copies(d):
        return (
            copy_to(
                colblk.at[fore],
                wbuf.at[row, col, fore, core],
                band1_s.at[0, d],
                band1_r.at[0, d],
                ctx=along_x(d),
            ),
            copy_to(
                colblk.at[rear],
                wbuf.at[row, col, rear, core],
                band1_s.at[1, d],
                band1_r.at[1, d],
                ctx=along_y(d),
            ),
        )

    def band2_copies(d):
        ahead, behind = wbuf.at[row, :, fore, core], wbuf.at[:, col, rear, core]
        return (
            copy_to(ahead, ahead, band2_s.at[0, d], band2_r.at[0, d], ctx=along_y(d)),
            copy_to(behind, behind, band2_s.at[1, d], band2_r.at[1, d], ctx=along_x(d)),
        )

    for d in range(1, side):
        for c in band1_copies(d):
            c.start()
    wbuf[row, col, :, core] = colblk[...]

    for h in range(heads):
        b = strength[h]
        gc = growth_col[h]
        k = keys[h]
        v = active(2 * heads + h)
        rhs = jnp.concatenate([(b * jnp.exp(gc)) * k, b * v], axis=1)
        sol = dot(inv[h], rhs).astype(BF16)
        solved[h] = sol
        kept = jnp.exp(last[h] - gc) * k
        both = dot(sol, kept, TN)
        at = (jnp.exp(last[h]) * eye - both[:HD, :]).astype(BF16)
        bt = both[HD:, :].astype(BF16)
        ab_send[h, :HD, :] = at
        ab_send[h, HD:, :] = bt

    def ab_copy(h):
        to = 2 * h + core
        return copy_to(ab_send.at[h], ab_recv.at[ctx], ab_s.at[h], ab_r.at[ctx], ctx=to)

    def ab_arrival(src):
        return copy_to(ab_send.at[0], ab_recv.at[src], ab_s.at[0], ab_r.at[src], ctx=src)

    def unless(skip, body):
        def step(i):
            @pl.when(i != skip)
            def _():
                body(i)

        return step

    mine = jnp.where(composer, ctx // 2, n_ctx)
    loop(0, heads, unless(mine, lambda h: ab_copy(h).start()))

    @pl.when(composer)
    def _():
        ab_recv[ctx] = ab_send[ctx // 2]

    for h in range(heads):
        gc = growth_col[h]
        q = queries[h]
        qk = decays[h] * dot(q, keys[h], NT)
        both = dot(qk, solved[h])
        qmap[h] = (jnp.exp(gc) * q - both[:, :HD]).astype(BF16)
        lout[h] = both[:, HD:]

    for d in range(1, side):
        for c in band1_copies(d):
            c.wait_send()
            c.wait_recv()
    for d in range(1, side):
        for c in band2_copies(d):
            c.start()

    def core_copies(d):
        r, q = (row + side - d) % side, (col + side - d) % side
        ahead, behind = wbuf.at[r, :, fore, core], wbuf.at[:, q, rear, core]
        return (
            copy_to(ahead, ahead, core_s.at[0, d], core_r.at[0, d], exp=sibling),
            copy_to(behind, behind, core_s.at[1, d], core_r.at[1, d], exp=sibling),
        )

    for c in core_copies(0):
        c.start()

    def st_copy(to):
        return copy_to(
            st_send.at[to], st_recv.at[ctx // 2], st_s.at[to], st_r.at[ctx // 2], ctx=to
        )

    @pl.when(composer)
    def _():
        loop(0, n_ctx, unless(ctx, lambda src: ab_arrival(src).wait_recv()))
        state = jnp.zeros((HD, HD), F32)
        for c in range(n_ctx):
            high = state.astype(BF16)
            st_send[c] = high
            if c < n_ctx - 1:
                low = (state - high.astype(F32)).astype(BF16)
                parts = dot(jnp.concatenate([high, low], axis=0), ab_recv[c, :HD, :])
                state = parts[:HD] + parts[HD:] + ab_recv[c, HD:, :].astype(F32)
        loop(0, n_ctx, unless(ctx, lambda to: st_copy(to).start()))
        st_recv[ctx // 2] = st_send[ctx]

    for d in range(1, side):
        for c, onward in zip(band2_copies(d), core_copies(d)):
            c.wait_send()
            c.wait_recv()
            onward.start()

    def st_arrival(h):
        src = 2 * h + core
        return copy_to(st_send.at[0], st_recv.at[h], st_s.at[0], st_r.at[h], ctx=src)

    loop(0, heads, unless(mine, lambda h: st_arrival(h).wait_recv()))
    loop(0, heads, unless(mine, lambda h: ab_copy(h).wait_send()))

    @pl.when(composer)
    def _():
        loop(0, n_ctx, unless(ctx, lambda to: st_copy(to).wait_send()))

    for d in range(1, side):
        for c in w1_copies(d):
            c.wait_send()
            c.wait_recv()
    for c in owns:
        c.wait()
    for d in range(1, side):
        for c in w2_copies(d):
            c.start()

    for c in loads[5:]:
        c.wait()
    gain = gain_ref[...]
    for h in range(heads):
        read = dot(qmap[h], st_recv[h], NT) + lout[h]
        scale = lax.rsqrt(jnp.mean(read * read, axis=-1, keepdims=True) + EPS)
        z = z_ref[:, h * HD : (h + 1) * HD].astype(F32)
        normed[:, h * HD : (h + 1) * HD] = (read * scale * gain * silu(z)).astype(BF16)

    for d in range(side):
        for c in core_copies(d):
            c.wait_send()
            c.wait_recv()

    squares = jnp.zeros((tokens, 1), F32)
    act = normed[...]
    for j in range(n_ctx):
        at = slice(j * lanes, (j + 1) * lanes)
        hid = (res_ref[:, at].astype(F32) + dot(act, wbuf[j // side, j % side].reshape(inner, lanes))).astype(BF16)
        hidden[:, at] = hid
        hid = hid.astype(F32)
        squares = squares + jnp.sum(hid * hid, axis=-1, keepdims=True)
    scale = lax.rsqrt(squares / model + EPS)
    routed_in = (hidden[...].astype(F32) * scale * post_ref[...]).astype(BF16)

    ids = column(ids_ref[...].astype(F32)).astype(jnp.int32)
    member = lax.broadcasted_iota(jnp.int32, (tokens, n_exp), 1) == ids
    member = member.astype(F32)
    ranks = dot(causal.astype(F32), member)
    slot = jnp.sum(ranks * member, axis=1, keepdims=True).astype(jnp.int32) - 1
    first = ids * (2 * cap) + slot
    places = lax.broadcasted_iota(jnp.int32, (tokens, 2 * cap * n_exp), 1)
    pick_low = (places == first).astype(F32).astype(BF16)
    pick_high = (places == first + cap).astype(F32).astype(BF16)
    sent = dot(pick_low, routed_in[:, :halfm], TN) + dot(pick_high, routed_in[:, halfm:], TN)
    outbound[...] = sent.astype(BF16).reshape(outbound.shape)

    def out_copy(d):
        to = (exp + d) % n_exp
        return copy_to(outbound.at[to], arrived.at[exp], out_s.at[d], out_r.at[d], exp=to)

    loop(1, n_exp, lambda d: out_copy(d).start())
    arrived[exp] = outbound[exp]

    for d in range(1, side):
        for c in w2_copies(d):
            c.wait_send()
            c.wait_recv()

    def out_wait(d):
        c = out_copy(d)
        c.wait_send()
        c.wait_recv()

    loop(1, n_exp, out_wait)

    ff = wg_ref.shape[1]
    came = arrived[...].astype(F32)
    rows_in = jnp.concatenate(
        [
            came[:, :cap, :].reshape(n_exp * cap, halfm),
            came[:, cap:, :].reshape(n_exp * cap, halfm),
        ],
        axis=1,
    ).astype(BF16)
    gate_part = dot(rows_in, gate_full[...].reshape(model, ff))
    up_part = dot(rows_in, up_full[...].reshape(model, ff))
    activated = (silu(gate_part) * up_part).astype(BF16)
    blocks = n_ctx // 2
    for j in range(blocks):
        parts = []
        for i in (j, j + blocks):
            down = jnp.concatenate(
                [down_full[0, i // side, i % side], down_full[1, i // side, i % side]], axis=0
            )
            parts.append(dot(activated, down).reshape(n_exp, cap, lanes))
        answer[:, :, j * lanes : (j + 1) * lanes] = jnp.concatenate(parts, axis=1).astype(BF16)

    def back_copy(d):
        to = (exp + d) % n_exp
        return copy_to(answer.at[to], returned.at[exp], back_s.at[d], back_r.at[d], exp=to)

    loop(1, n_exp, lambda d: back_copy(d).start())
    returned[exp] = answer[exp]

    def back_wait(d):
        c = back_copy(d)
        c.wait_send()
        c.wait_recv()

    loop(1, n_exp, back_wait)

    back = returned[...].reshape(2 * cap * n_exp, halfm)
    weight = column(rw_ref[...])
    for pick, at in ((pick_low, slice(0, halfm)), (pick_high, slice(halfm, model))):
        fetched = dot(pick, back)
        out_ref[:, at] = (hidden[:, at].astype(F32) + weight * fetched).astype(BF16)


def on_device(n_ctx, n_exp, *args):
    (qkv, taps, lgate, beta, z, gain, ow, res, post, ids, rw, wg, wu, wd) = args
    tokens, width = qkv.shape[1:]
    heads = lgate.shape[2]
    model = res.shape[2]
    ff = wg.shape[2]
    side = math.isqrt(n_ctx)
    cap = 2 * ids.shape[2] * tokens // n_exp
    inner = heads * HD
    lanes = ow.shape[1]
    chips = n_exp // 2
    sem = pltpu.SemaphoreType.DMA
    operands = (
        qkv[0],
        taps,
        lgate[0].T,
        beta[0].T,
        z[0],
        gain[None],
        ow,
        res[0],
        post[None],
        ids[0].T,
        rw[0].T,
        wg[0],
        wu[0],
        wd[0],
    )
    slots = (n_exp, 2 * cap, model // 2)
    scratch = [pltpu.VMEM(x.shape, x.dtype) for x in operands[:11]]
    scratch += [
        pltpu.VMEM((HALO, width), BF16),
        pltpu.VMEM((8 + tokens, width), F32),
        pltpu.VMEM((heads, tokens, HD), F32),
        pltpu.VMEM((heads, tokens, HD), F32),
        pltpu.VMEM((heads, tokens, tokens), F32),
        pltpu.VMEM((heads, tokens, 2 * HD), BF16),
        pltpu.VMEM((heads, 2 * HD, HD), BF16),
        pltpu.VMEM((n_ctx, 2 * HD, HD), BF16),
        pltpu.VMEM((n_ctx, HD, HD), BF16),
        pltpu.VMEM((heads, HD, HD), BF16),
        pltpu.VMEM((heads, tokens, HD), BF16),
        pltpu.VMEM((heads, tokens, HD), F32),
        pltpu.VMEM((tokens, inner), BF16),
        pltpu.VMEM((chips, ow.shape[0], lanes), BF16),
        pltpu.VMEM((side, side, chips, 2, ow.shape[0], lanes), BF16),
        pltpu.VMEM((tokens, model), BF16),
        pltpu.VMEM((side, side, model // n_ctx, ff), BF16),
        pltpu.VMEM((side, side, model // n_ctx, ff), BF16),
        pltpu.VMEM((2, side, side, ff // 2, lanes), BF16),
        pltpu.VMEM(slots, BF16),
        pltpu.VMEM(slots, BF16),
        pltpu.VMEM(slots, BF16),
        pltpu.VMEM(slots, BF16),
        sem((11,)),
        sem((4,)),
        sem((1,)),
        sem((1,)),
        sem((chips,)),
        sem((chips,)),
        sem((2, side)),
        sem((2, side)),
        sem((2, side)),
        sem((2, side)),
        sem((2, side)),
        sem((2, side)),
        sem((heads,)),
        sem((n_ctx,)),
        sem((n_ctx,)),
        sem((heads,)),
        sem((4, side)),
        sem((4, side)),
        sem((4, side)),
        sem((4, side)),
        sem((n_exp,)),
        sem((n_exp,)),
        sem((n_exp,)),
        sem((n_exp,)),
    ]
    out = pl.pallas_call(
        functools.partial(kernel, n_ctx, n_exp, side),
        out_shape=jax.ShapeDtypeStruct((tokens, model), BF16),
        in_specs=[pl.BlockSpec(memory_space=pltpu.HBM)] * 14,
        out_specs=pl.BlockSpec(memory_space=pltpu.VMEM),
        scratch_shapes=scratch,
        compiler_params=pltpu.CompilerParams(
            collective_id=0, has_side_effects=True, vmem_limit_bytes=63 * 2**20
        ),
    )(*operands)
    return out[None]


def solution(mesh):
    placed = (
        P("exp", "ctx", None),
        P(),
        P("exp", "ctx", None),
        P("exp", "ctx", None),
        P("exp", "ctx", None),
        P(),
        P("exp", "ctx"),
        P("exp", "ctx", None),
        P(),
        P("exp", "ctx", None),
        P("exp", "ctx", None),
        P("exp", "ctx", None),
        P("exp", "ctx", None),
        P("exp", None, "ctx"),
    )
    return jax.shard_map(
        functools.partial(on_device, mesh.shape["ctx"], mesh.shape["exp"]),
        mesh=mesh,
        in_specs=placed,
        out_specs=P("exp", "ctx", None),
        check_vma=False,
    )
```

```python
import functools
import math

import jax
import jax.numpy as jnp
from jax import lax
from jax.experimental import pallas as pl
from jax.experimental.pallas import tpu as pltpu
from jax.sharding import PartitionSpec as P

MESH = pl.DeviceIdType.MESH
F32, BF16 = jnp.float32, jnp.bfloat16
NN, NT, TN = ((1,), (0,)), ((1,), (1,)), ((0,), (0,))
EPS = 1e-06
HD = 128
HALO = 16


def dot(a, b, dims=NN):
    return lax.dot_general(
        a.astype(BF16), b.astype(BF16), (dims, ((), ())), preferred_element_type=F32
    )


def silu(u):
    return u / (1.0 + jnp.exp(-u))


def copy_to(src, dst, send, recv, **where):
    return pltpu.make_async_remote_copy(
        src_ref=src,
        dst_ref=dst,
        send_sem=send,
        recv_sem=recv,
        device_id=where,
        device_id_type=MESH,
    )


def loop(low, high, body):
    lax.fori_loop(low, high, lambda i, c: (body(i), c)[1], 0)


def kernel(
    n_ctx,
    n_exp,
    side,
    qkv_hbm,
    taps_hbm,
    lgate_hbm,
    beta_hbm,
    z_hbm,
    gain_hbm,
    ow_hbm,
    res_hbm,
    post_hbm,
    ids_hbm,
    rw_hbm,
    wg_ref,
    wu_ref,
    wd_ref,
    out_ref,
    qkv_ref,
    taps_ref,
    lgate_ref,
    beta_ref,
    z_ref,
    gain_ref,
    ow_ref,
    res_ref,
    post_ref,
    ids_ref,
    rw_ref,
    halo,
    xs,
    keys,
    queries,
    decays,
    solved,
    ab_send,
    ab_recv,
    st_send,
    st_recv,
    qmap,
    lout,
    normed,
    colblk,
    wbuf,
    hidden,
    gate_full,
    up_full,
    down_full,
    outbound,
    arrived,
    answer,
    returned,
    copy_gate,
    copy_up,
    copy_down,
    row_gate,
    row_down,
    col_up,
    col_down,
    load_s,
    own_s,
    zx_s,
    zx_r,
    halo_s,
    halo_r,
    col_s,
    col_r,
    band1_s,
    band1_r,
    band2_s,
    band2_r,
    core_s,
    core_r,
    ab_s,
    ab_r,
    st_s,
    st_r,
    g1_s,
    g1_r,
    u1_s,
    u1_r,
    g2_s,
    g2_r,
    u2_s,
    u2_r,
    pair_s,
    pair_r,
    out_s,
    out_r,
    back_s,
    back_r,
):
    ctx, exp = lax.axis_index("ctx"), lax.axis_index("exp")
    row, col = ctx // side, ctx % side
    tokens, width = qkv_ref.shape
    heads = width // (3 * HD)
    inner = heads * HD
    model = res_ref.shape[1]
    halfm = model // 2
    lanes = ow_ref.shape[1]
    slab = ow_ref.shape[0]
    cap = outbound.shape[1] // 2
    wrows = wg_ref.shape[0]
    chip, core = exp // 2, exp % 2
    chips = n_exp // 2
    sibling = exp + 1 - 2 * core
    composer = ctx % 2 == core

    after = chips // 8
    before = chips // 2 - 1 - after
    away = 2 * after + 1
    second, odd = col % 2, row % 2
    up = 1 - 2 * core
    my_up = 1 - 2 * odd
    my_expert = 2 * ((chip + chips - second * away * my_up) % chips) + odd
    reach = jnp.where(second == 0, before, after)
    my_block = reach * 4 + odd * 2 + second

    barrier = pltpu.get_barrier_semaphore()

    def greet(to_ctx, to_exp):
        pl.semaphore_signal(
            barrier, inc=1, device_id={"ctx": to_ctx, "exp": to_exp}, device_id_type=MESH
        )

    def beside(j):
        return (row - odd + j // 2) * side + col - second + j % 2

    corner = odd * 2 + second
    loop(1, n_ctx, lambda d: greet((ctx + d) % n_ctx, exp))
    loop(0, n_ctx, lambda d: greet((ctx + d) % n_ctx, sibling))
    loop(1, chips, lambda d: greet(ctx, (exp + 2 * d) % n_exp))
    for j in range(4):

        @pl.when(j != corner)
        def _():
            loop(1, before + 1, lambda d: greet(beside(j), (exp + 2 * d) % n_exp))
            loop(1, before + 1, lambda d: greet(beside(j), (exp + n_exp - 2 * d) % n_exp))

    greeted = 2 * n_ctx - 1 + chips - 1 + 6 * before
    loads = [
        pltpu.make_async_copy(src, dst, load_s.at[i])
        for i, (src, dst) in enumerate(
            (
                (qkv_hbm, qkv_ref),
                (taps_hbm, taps_ref),
                (lgate_hbm, lgate_ref),
                (beta_hbm, beta_ref),
                (ow_hbm, ow_ref),
                (z_hbm, z_ref),
                (gain_hbm, gain_ref),
                (res_hbm, res_ref),
                (post_hbm, post_ref),
                (ids_hbm, ids_ref),
                (rw_hbm, rw_ref),
            )
        )
    ]
    for c in loads:
        c.start()
    half_ff = wd_ref.shape[0] // 2
    wd_first, wd_last = wd_ref.at[pl.ds(0, half_ff), :], wd_ref.at[pl.ds(half_ff, half_ff), :]
    cd_first = copy_down.at[pl.ds(0, half_ff), :]
    cd_last = copy_down.at[pl.ds(half_ff, half_ff), :]
    own_row = [
        pltpu.make_async_copy(wg_ref, row_gate.at[col], own_s.at[0]),
        pltpu.make_async_copy(wd_first, row_down.at[col], own_s.at[1]),
    ]
    own_col = [
        pltpu.make_async_copy(wu_ref, col_up.at[0, row], own_s.at[2]),
        pltpu.make_async_copy(wd_last, col_down.at[0, row], own_s.at[3]),
    ]

    @pl.when(second == 0)
    def _():
        for c in own_row:
            c.start()

    @pl.when(odd == core)
    def _():
        for c in own_col:
            c.start()

    for c in loads[:5]:
        c.wait()
    xs[8:, :] = qkv_ref[...].astype(F32)
    pl.semaphore_wait(barrier, greeted)

    halo_copy = copy_to(
        qkv_ref.at[pl.ds(tokens - HALO, HALO), :],
        halo,
        halo_s.at[0],
        halo_r.at[0],
        ctx=(ctx + 1) % n_ctx,
    )
    halo_copy.start()

    def col_copy(d):
        return copy_to(
            ow_ref, colblk.at[chip], col_s.at[d], col_r.at[d], exp=(exp + 2 * d) % n_exp
        )

    loop(1, chips, lambda d: col_copy(d).start())
    colblk[chip] = ow_ref[...]

    def along_x(d):
        return row * side + (col + d) % side

    def along_y(d):
        return ((row + d) % side) * side + col

    away_exp = 2 * ((chip + chips + away * up) % chips) + core
    zx_copies = [
        copy_to(src, dst, zx_s.at[i], zx_r.at[i], exp=away_exp)
        for i, (src, dst) in enumerate(
            ((wg_ref, copy_gate), (wu_ref, copy_up), (wd_ref, copy_down))
        )
    ]

    def unless(skip, body):
        def step(i):
            @pl.when(i != skip)
            def _():
                body(i)

        return step

    def g1_copies(kind, to):
        gate, down = ((wg_ref, wd_first), (copy_gate, cd_first))[kind]
        there = row * side + to
        return (
            copy_to(gate, row_gate.at[col], g1_s.at[0, to], g1_r.at[0, col], ctx=there),
            copy_to(down, row_down.at[col], g1_s.at[1, to], g1_r.at[1, col], ctx=there),
        )

    def g1_arrivals(src):
        there = row * side + src
        return (
            copy_to(wg_ref, row_gate.at[src], g1_s.at[0, src], g1_r.at[0, src], ctx=there),
            copy_to(wd_first, row_down.at[src], g1_s.at[1, src], g1_r.at[1, src], ctx=there),
        )

    def u1_copies(kind, j):
        up_src, down = ((wu_ref, wd_last), (copy_up, cd_last))[kind]
        there = (core + 2 * j) * side + col
        return (
            copy_to(
                up_src, col_up.at[kind, row], u1_s.at[0, kind, j], u1_r.at[0, kind, row], ctx=there
            ),
            copy_to(
                down, col_down.at[kind, row], u1_s.at[1, kind, j], u1_r.at[1, kind, row], ctx=there
            ),
        )

    def u1_arrivals(kind, src):
        there = src * side + col
        return (
            copy_to(
                wu_ref, col_up.at[kind, src], u1_s.at[0, kind, 0], u1_r.at[0, kind, src], ctx=there
            ),
            copy_to(
                wd_last,
                col_down.at[kind, src],
                u1_s.at[1, kind, 0],
                u1_r.at[1, kind, src],
                ctx=there,
            ),
        )

    halves = side // 2
    row_own = jnp.where(odd == core, row // 2, halves)

    def start_all(copies):
        for c in copies:
            c.start()

    def wait_sent(copies):
        for c in copies:
            c.wait_send()

    def wait_came(copies):
        for c in copies:
            c.wait_recv()

    def each_first(kind, act):
        for j in range(halves):
            to = 2 * j + kind

            @pl.when(to != col)
            def _():
                act(g1_copies(kind, to))

            @pl.when(j != row_own)
            def _():
                act(u1_copies(kind, j))

    start_all(zx_copies)
    each_first(0, start_all)

    tri_r = lax.broadcasted_iota(jnp.int32, (tokens, tokens), 0)
    tri_c = lax.broadcasted_iota(jnp.int32, (tokens, tokens), 1)
    causal = tri_r >= tri_c
    strict = tri_r > tri_c
    eye = (tri_r == tri_c).astype(F32)
    growth_row = lax.dot_general(
        lgate_ref[...],
        (tri_r <= tri_c).astype(F32),
        (NN, ((), ())),
        preferred_element_type=F32,
        precision=lax.Precision.HIGHEST,
    )

    def column(line):
        return jnp.sum(line * eye, axis=1, keepdims=True)

    growth = [growth_row[h : h + 1, :] for h in range(heads)]
    growth_col = [column(g) for g in growth]
    last = [g[:, tokens - 1 :] for g in growth]
    strength = [column(beta_ref[h : h + 1, :]) for h in range(heads)]
    halo_copy.wait()
    xs[:8, :] = jnp.where(ctx > 0, halo[...].astype(F32)[HALO - 8 :, :], 0.0)
    taps = taps_ref[...].astype(F32)

    def active(block):
        at = slice(block * HD, (block + 1) * HD)
        total = xs[5 : 5 + tokens, at] * taps[0:1, at]
        for j in range(1, 4):
            total = total + xs[5 + j : 5 + j + tokens, at] * taps[j : j + 1, at]
        return silu(total)

    def unit(rows):
        return rows * lax.rsqrt(jnp.sum(rows * rows, axis=-1, keepdims=True) + EPS)

    lowers = []
    for h in range(heads):
        q = unit(active(h)) * HD ** (-0.5)
        k = unit(active(heads + h))
        queries[h] = q
        keys[h] = k
        gc, gr = growth_col[h], growth[h]
        decay = jnp.where(causal, jnp.exp(jnp.where(causal, gc - gr, 0.0)), 0.0)
        decays[h] = decay
        kk = dot(k, k, NT)
        lowers.append(jnp.where(strict, strength[h] * decay * kk, 0.0))

    def same(size):
        return tri_r // size == tri_c // size

    base = 16
    near = same(base)
    power = [jnp.where(near, l, 0.0) for l in lowers]
    inv = [eye - p for p in power]
    for _ in range(3):
        power = [dot(p, p) for p in power]
        inv = [x + dot(x, p) for x, p in zip(inv, power)]
    size = base
    while size < tokens:
        ring = jnp.logical_and(same(2 * size), jnp.logical_not(same(size)))
        mid = [dot(jnp.where(ring, l, 0.0), x) for l, x in zip(lowers, inv)]
        inv = [x - dot(x, m) for x, m in zip(inv, mid)]
        size *= 2

    def col_wait(d):
        c = col_copy(d)
        c.wait_send()
        c.wait_recv()

    loop(1, chips, col_wait)
    fore, rear = pl.ds(0, chips // 2), pl.ds(chips // 2, chips // 2)

    def band1_copies(d):
        return (
            copy_to(
                colblk.at[fore],
                wbuf.at[row, col, fore, core],
                band1_s.at[0, d],
                band1_r.at[0, d],
                ctx=along_x(d),
            ),
            copy_to(
                colblk.at[rear],
                wbuf.at[row, col, rear, core],
                band1_s.at[1, d],
                band1_r.at[1, d],
                ctx=along_y(d),
            ),
        )

    def band2_copies(d):
        ahead, behind = wbuf.at[row, :, fore, core], wbuf.at[:, col, rear, core]
        return (
            copy_to(ahead, ahead, band2_s.at[0, d], band2_r.at[0, d], ctx=along_y(d)),
            copy_to(behind, behind, band2_s.at[1, d], band2_r.at[1, d], ctx=along_x(d)),
        )

    for d in range(1, side):
        for c in band1_copies(d):
            c.start()
    wbuf[row, col, :, core] = colblk[...]

    for h in range(heads):
        b = strength[h]
        gc = growth_col[h]
        k = keys[h]
        v = active(2 * heads + h)
        rhs = jnp.concatenate([(b * jnp.exp(gc)) * k, b * v], axis=1)
        sol = dot(inv[h], rhs).astype(BF16)
        solved[h] = sol
        kept = jnp.exp(last[h] - gc) * k
        both = dot(sol, kept, TN)
        at = (jnp.exp(last[h]) * eye - both[:HD, :]).astype(BF16)
        bt = both[HD:, :].astype(BF16)
        ab_send[h, :HD, :] = at
        ab_send[h, HD:, :] = bt

    def ab_copy(h):
        to = 2 * h + core
        return copy_to(ab_send.at[h], ab_recv.at[ctx], ab_s.at[h], ab_r.at[ctx], ctx=to)

    def ab_arrival(src):
        return copy_to(ab_send.at[0], ab_recv.at[src], ab_s.at[0], ab_r.at[src], ctx=src)

    mine = jnp.where(composer, ctx // 2, n_ctx)
    loop(0, heads, unless(mine, lambda h: ab_copy(h).start()))

    @pl.when(composer)
    def _():
        ab_recv[ctx] = ab_send[ctx // 2]

    for h in range(heads):
        gc = growth_col[h]
        q = queries[h]
        qk = decays[h] * dot(q, keys[h], NT)
        both = dot(qk, solved[h])
        qmap[h] = (jnp.exp(gc) * q - both[:, :HD]).astype(BF16)
        lout[h] = both[:, HD:]

    for d in range(1, side):
        for c in band1_copies(d):
            c.wait_send()
            c.wait_recv()
    for d in range(1, side):
        for c in band2_copies(d):
            c.start()

    def core_copies(d):
        r, q = (row + side - d) % side, (col + side - d) % side
        ahead, behind = wbuf.at[r, :, fore, core], wbuf.at[:, q, rear, core]
        return (
            copy_to(ahead, ahead, core_s.at[0, d], core_r.at[0, d], exp=sibling),
            copy_to(behind, behind, core_s.at[1, d], core_r.at[1, d], exp=sibling),
        )

    for c in core_copies(0):
        c.start()

    def st_copy(to):
        return copy_to(
            st_send.at[to], st_recv.at[ctx // 2], st_s.at[to], st_r.at[ctx // 2], ctx=to
        )

    @pl.when(composer)
    def _():
        loop(0, n_ctx, unless(ctx, lambda src: ab_arrival(src).wait_recv()))
        state = jnp.zeros((HD, HD), F32)
        for c in range(n_ctx):
            high = state.astype(BF16)
            st_send[c] = high
            if c < n_ctx - 1:
                low = (state - high.astype(F32)).astype(BF16)
                parts = dot(jnp.concatenate([high, low], axis=0), ab_recv[c, :HD, :])
                state = parts[:HD] + parts[HD:] + ab_recv[c, HD:, :].astype(F32)
        loop(0, n_ctx, unless(ctx, lambda to: st_copy(to).start()))
        st_recv[ctx // 2] = st_send[ctx]

    for c in zx_copies:
        c.wait_recv()
    each_first(1, start_all)

    @pl.when(second == 0)
    def _():
        for c in own_row:
            c.wait()

    @pl.when(second == 1)
    def _():
        row_gate[col] = copy_gate[...]
        row_down[col] = copy_down[:half_ff, :]

    @pl.when(odd == core)
    def _():
        for c in own_col:
            c.wait()
        col_up[1, row] = copy_up[...]
        col_down[1, row] = copy_down[half_ff:, :]

    for d in range(1, side):
        for c, onward in zip(band2_copies(d), core_copies(d)):
            c.wait_send()
            c.wait_recv()
            onward.start()

    def st_arrival(h):
        src = 2 * h + core
        return copy_to(st_send.at[0], st_recv.at[h], st_s.at[0], st_r.at[h], ctx=src)

    loop(0, heads, unless(mine, lambda h: st_arrival(h).wait_recv()))
    loop(0, heads, unless(mine, lambda h: ab_copy(h).wait_send()))

    @pl.when(composer)
    def _():
        loop(0, n_ctx, unless(ctx, lambda to: st_copy(to).wait_send()))

    def g2_copies(j):
        there = (core + 2 * j) * side + col
        return (
            copy_to(
                row_gate, gate_full.at[row], g2_s.at[0, j], g2_r.at[0, row], ctx=there, exp=2 * chip
            ),
            copy_to(
                row_down,
                down_full.at[0, row],
                g2_s.at[1, j],
                g2_r.at[1, row],
                ctx=there,
                exp=2 * chip,
            ),
        )

    def g2_arrivals(src):
        there = src * side + col
        return (
            copy_to(
                row_gate,
                gate_full.at[src],
                g2_s.at[0, 0],
                g2_r.at[0, src],
                ctx=there,
                exp=2 * chip + odd,
            ),
            copy_to(
                row_down,
                down_full.at[0, src],
                g2_s.at[1, 0],
                g2_r.at[1, src],
                ctx=there,
                exp=2 * chip + odd,
            ),
        )

    def u2_copies(kind, j):
        there = row * side + 2 * j + kind
        return (
            copy_to(
                col_up.at[kind],
                up_full.at[:, col],
                u2_s.at[0, kind, j],
                u2_r.at[0, col],
                ctx=there,
                exp=2 * chip + 1,
            ),
            copy_to(
                col_down.at[kind],
                down_full.at[1, :, col],
                u2_s.at[1, kind, j],
                u2_r.at[1, col],
                ctx=there,
                exp=2 * chip + 1,
            ),
        )

    def u2_arrivals(src):
        there = row * side + src
        return (
            copy_to(
                col_up.at[0],
                up_full.at[:, src],
                u2_s.at[0, 0, 0],
                u2_r.at[0, src],
                ctx=there,
                exp=2 * chip + odd,
            ),
            copy_to(
                col_down.at[0],
                down_full.at[1, :, src],
                u2_s.at[1, 0, 0],
                u2_r.at[1, src],
                ctx=there,
                exp=2 * chip + odd,
            ),
        )

    g2_own = jnp.where(jnp.logical_and(core == 0, odd == 0), row // 2, halves)
    u2_own = jnp.where(jnp.logical_and(core == 1, odd == 1), col, side)

    def each_second(act):
        for j in range(halves):

            @pl.when(j != g2_own)
            def _():
                act(g2_copies(j))

        @pl.when(odd == core)
        def _():
            for kind in range(2):
                for j in range(halves):

                    @pl.when(2 * j + kind != u2_own)
                    def _():
                        act(u2_copies(kind, j))

    loop(0, side, unless(col, lambda src: wait_came(g1_arrivals(src))))

    @pl.when(odd == core)
    def _():
        for kind in range(2):
            loop(0, side, unless(row, lambda src: wait_came(u1_arrivals(kind, src))))

    each_second(start_all)

    @pl.when(g2_own < halves)
    def _():
        gate_full[row] = row_gate[...]
        down_full[0, row] = row_down[...]

    @pl.when(u2_own < side)
    def _():
        for r in range(side):
            up_full[r, col] = col_up[second, r]
            down_full[1, r, col] = col_down[second, r]

    for c in loads[5:]:
        c.wait()
    gain = gain_ref[...]
    for h in range(heads):
        read = dot(qmap[h], st_recv[h], NT) + lout[h]
        scale = lax.rsqrt(jnp.mean(read * read, axis=-1, keepdims=True) + EPS)
        z = z_ref[:, h * HD : (h + 1) * HD].astype(F32)
        normed[:, h * HD : (h + 1) * HD] = (read * scale * gain * silu(z)).astype(BF16)

    for d in range(side):
        for c in core_copies(d):
            c.wait_send()
            c.wait_recv()

    squares = jnp.zeros((tokens, 1), F32)
    act = normed[...]
    for j in range(n_ctx):
        at = slice(j * lanes, (j + 1) * lanes)
        hid = (res_ref[:, at].astype(F32) + dot(act, wbuf[j // side, j % side].reshape(inner, lanes))).astype(BF16)
        hidden[:, at] = hid
        hid = hid.astype(F32)
        squares = squares + jnp.sum(hid * hid, axis=-1, keepdims=True)
    scale = lax.rsqrt(squares / model + EPS)
    routed_in = (hidden[...].astype(F32) * scale * post_ref[...]).astype(BF16)

    ids = column(ids_ref[...].astype(F32)).astype(jnp.int32)
    member = lax.broadcasted_iota(jnp.int32, (tokens, n_exp), 1) == ids
    member = member.astype(F32)
    ranks = dot(causal.astype(F32), member)
    slot = jnp.sum(ranks * member, axis=1, keepdims=True).astype(jnp.int32) - 1
    first = ids * (2 * cap) + slot
    places = lax.broadcasted_iota(jnp.int32, (tokens, 2 * cap * n_exp), 1)
    pick_low = (places == first).astype(F32).astype(BF16)
    pick_high = (places == first + cap).astype(F32).astype(BF16)
    sent = dot(pick_low, routed_in[:, :halfm], TN) + dot(pick_high, routed_in[:, halfm:], TN)
    outbound[...] = sent.astype(BF16).reshape(outbound.shape)

    def out_copy(k, c):
        rise = 1 - 2 * c
        place = (-k * rise) % chips
        spread = (place + before) % chips
        if spread < chips // 2:
            kind, shift = 0, k % chips
        else:
            kind, shift, spread = 1, (k + away * rise) % chips, spread - chips // 2
        to_ctx = (row - odd + c) * side + col - second + kind
        to_exp = (exp + 2 * shift) % n_exp
        block = spread * 4 + odd * 2 + second
        what = copy_to(
            outbound.at[(2 * chip + 2 * k) % n_exp + c],
            arrived.at[block],
            out_s.at[2 * k + c],
            out_r.at[block],
            ctx=to_ctx,
            exp=to_exp,
        )
        if shift:
            return what, None
        return what, jnp.logical_and(odd == c, second == kind)

    def each_out(act):
        for k in range(chips):
            for c in range(2):
                what, here = out_copy(k, c)
                if here is None:
                    act([what])
                else:

                    @pl.when(jnp.logical_not(here))
                    def _():
                        act([what])

    each_out(start_all)
    arrived[my_block] = outbound[my_expert]

    def pair_copies(i, which):
        parts = (
            (gate_full.at[i], down_full.at[0, i]),
            (up_full.at[:, i], down_full.at[1, :, i]),
        )[which]
        return [
            copy_to(
                part, part, pair_s.at[2 * which + n, i], pair_r.at[2 * which + n, i], exp=sibling
            )
            for n, part in enumerate(parts)
        ]

    @pl.when(core == 0)
    def _():
        def onward(src):
            @pl.when(jnp.logical_or(src != row, odd == 1))
            def _():
                wait_came(g2_arrivals(src))

            start_all(pair_copies(src, 0))

        loop(0, side, onward)

    @pl.when(core == 1)
    def _():
        def onward(src):
            @pl.when(jnp.logical_or(src != col, odd == 0))
            def _():
                wait_came(u2_arrivals(src))

            start_all(pair_copies(src, 1))

        loop(0, side, onward)

    wait_sent(zx_copies)
    each_first(0, wait_sent)
    each_first(1, wait_sent)
    each_second(wait_sent)

    @pl.when(core == 0)
    def _():
        for i in range(side):
            wait_sent(pair_copies(i, 0))
            wait_came(pair_copies(i, 1))

    @pl.when(core == 1)
    def _():
        for i in range(side):
            wait_sent(pair_copies(i, 1))
            wait_came(pair_copies(i, 0))

    def out_arrival(block):
        return copy_to(
            outbound.at[0], arrived.at[block], out_s.at[0], out_r.at[block], exp=sibling
        )

    loop(0, n_exp, unless(my_block, lambda block: out_arrival(block).wait_recv()))
    each_out(wait_sent)

    ff = wg_ref.shape[1]
    came = arrived[...].astype(F32)
    rows_in = jnp.concatenate(
        [
            came[:, :cap, :].reshape(n_exp * cap, halfm),
            came[:, cap:, :].reshape(n_exp * cap, halfm),
        ],
        axis=1,
    ).astype(BF16)
    gate_part = dot(rows_in, gate_full[...].reshape(model, ff))
    up_part = dot(rows_in, up_full[...].reshape(model, ff))
    activated = (silu(gate_part) * up_part).astype(BF16)
    blocks = n_ctx // 2
    for j in range(blocks):
        parts = []
        for i in (j, j + blocks):
            down = jnp.concatenate(
                [down_full[0, i // side, i % side], down_full[1, i // side, i % side]], axis=0
            )
            parts.append(dot(activated, down).reshape(n_exp, cap, lanes))
        answer[:, :, j * lanes : (j + 1) * lanes] = jnp.concatenate(parts, axis=1).astype(BF16)

    def back_copy(block):
        far = (block // 4 + chips - reach) * my_up + 2 * chips
        return copy_to(
            answer.at[block],
            returned.at[my_expert],
            back_s.at[block],
            back_r.at[my_expert],
            ctx=beside(block % 4),
            exp=2 * ((chip + far) % chips) + core,
        )

    def back_arrival(expert):
        return copy_to(
            answer.at[0], returned.at[expert], back_s.at[0], back_r.at[expert], exp=sibling
        )

    loop(0, n_exp, unless(my_block, lambda block: back_copy(block).start()))
    returned[my_expert] = answer[my_block]
    loop(0, n_exp, unless(my_expert, lambda expert: back_arrival(expert).wait_recv()))
    loop(0, n_exp, unless(my_block, lambda block: back_copy(block).wait_send()))

    back = returned[...].reshape(2 * cap * n_exp, halfm)
    weight = column(rw_ref[...])
    for pick, at in ((pick_low, slice(0, halfm)), (pick_high, slice(halfm, model))):
        fetched = dot(pick, back)
        out_ref[:, at] = (hidden[:, at].astype(F32) + weight * fetched).astype(BF16)


def on_device(n_ctx, n_exp, *args):
    (qkv, taps, lgate, beta, z, gain, ow, res, post, ids, rw, wg, wu, wd) = args
    tokens, width = qkv.shape[1:]
    heads = lgate.shape[2]
    model = res.shape[2]
    ff = wg.shape[2]
    side = math.isqrt(n_ctx)
    cap = 2 * ids.shape[2] * tokens // n_exp
    inner = heads * HD
    lanes = ow.shape[1]
    chips = n_exp // 2
    sem = pltpu.SemaphoreType.DMA
    operands = (
        qkv[0],
        taps,
        lgate[0].T,
        beta[0].T,
        z[0],
        gain[None],
        ow,
        res[0],
        post[None],
        ids[0].T,
        rw[0].T,
        wg[0],
        wu[0],
        wd[0],
    )
    slots = (n_exp, 2 * cap, model // 2)
    scratch = [pltpu.VMEM(x.shape, x.dtype) for x in operands[:11]]
    scratch += [
        pltpu.VMEM((HALO, width), BF16),
        pltpu.VMEM((8 + tokens, width), F32),
        pltpu.VMEM((heads, tokens, HD), F32),
        pltpu.VMEM((heads, tokens, HD), F32),
        pltpu.VMEM((heads, tokens, tokens), F32),
        pltpu.VMEM((heads, tokens, 2 * HD), BF16),
        pltpu.VMEM((heads, 2 * HD, HD), BF16),
        pltpu.VMEM((n_ctx, 2 * HD, HD), BF16),
        pltpu.VMEM((n_ctx, HD, HD), BF16),
        pltpu.VMEM((heads, HD, HD), BF16),
        pltpu.VMEM((heads, tokens, HD), BF16),
        pltpu.VMEM((heads, tokens, HD), F32),
        pltpu.VMEM((tokens, inner), BF16),
        pltpu.VMEM((chips, ow.shape[0], lanes), BF16),
        pltpu.VMEM((side, side, chips, 2, ow.shape[0], lanes), BF16),
        pltpu.VMEM((tokens, model), BF16),
        pltpu.VMEM((side, side, model // n_ctx, ff), BF16),
        pltpu.VMEM((side, side, model // n_ctx, ff), BF16),
        pltpu.VMEM((2, side, side, ff // 2, lanes), BF16),
        pltpu.VMEM(slots, BF16),
        pltpu.VMEM(slots, BF16),
        pltpu.VMEM(slots, BF16),
        pltpu.VMEM(slots, BF16),
        pltpu.VMEM((model // n_ctx, ff), BF16),
        pltpu.VMEM((model // n_ctx, ff), BF16),
        pltpu.VMEM((ff, lanes), BF16),
        pltpu.VMEM((side, model // n_ctx, ff), BF16),
        pltpu.VMEM((side, ff // 2, lanes), BF16),
        pltpu.VMEM((2, side, model // n_ctx, ff), BF16),
        pltpu.VMEM((2, side, ff // 2, lanes), BF16),
        sem((11,)),
        sem((4,)),
        sem((3,)),
        sem((3,)),
        sem((1,)),
        sem((1,)),
        sem((chips,)),
        sem((chips,)),
        sem((2, side)),
        sem((2, side)),
        sem((2, side)),
        sem((2, side)),
        sem((2, side)),
        sem((2, side)),
        sem((heads,)),
        sem((n_ctx,)),
        sem((n_ctx,)),
        sem((heads,)),
        sem((2, side)),
        sem((2, side)),
        sem((2, 2, side)),
        sem((2, 2, side)),
        sem((2, side)),
        sem((2, side)),
        sem((2, 2, side)),
        sem((2, side)),
        sem((4, side)),
        sem((4, side)),
        sem((n_exp,)),
        sem((n_exp,)),
        sem((n_exp,)),
        sem((n_exp,)),
    ]
    out = pl.pallas_call(
        functools.partial(kernel, n_ctx, n_exp, side),
        out_shape=jax.ShapeDtypeStruct((tokens, model), BF16),
        in_specs=[pl.BlockSpec(memory_space=pltpu.HBM)] * 14,
        out_specs=pl.BlockSpec(memory_space=pltpu.VMEM),
        scratch_shapes=scratch,
        compiler_params=pltpu.CompilerParams(
            collective_id=0, has_side_effects=True, vmem_limit_bytes=63 * 2**20
        ),
    )(*operands)
    return out[None]


def solution(mesh):
    placed = (
        P("exp", "ctx", None),
        P(),
        P("exp", "ctx", None),
        P("exp", "ctx", None),
        P("exp", "ctx", None),
        P(),
        P("exp", "ctx"),
        P("exp", "ctx", None),
        P(),
        P("exp", "ctx", None),
        P("exp", "ctx", None),
        P("exp", "ctx", None),
        P("exp", "ctx", None),
        P("exp", None, "ctx"),
    )
    return jax.shard_map(
        functools.partial(on_device, mesh.shape["ctx"], mesh.shape["exp"]),
        mesh=mesh,
        in_specs=placed,
        out_specs=P("exp", "ctx", None),
        check_vma=False,
    )
```

```python
import functools
import math

import jax
import jax.numpy as jnp
from jax import lax
from jax.experimental import pallas as pl
from jax.experimental.pallas import tpu as pltpu
from jax.sharding import PartitionSpec as P

MESH = pl.DeviceIdType.MESH
F32, BF16 = jnp.float32, jnp.bfloat16
NN, NT, TN = ((1,), (0,)), ((1,), (1,)), ((0,), (0,))
EPS = 1e-06
HD = 128
HALO = 16


def dot(a, b, dims=NN):
    return lax.dot_general(
        a.astype(BF16), b.astype(BF16), (dims, ((), ())), preferred_element_type=F32
    )


def silu(u):
    return u / (1.0 + jnp.exp(-u))


def copy_to(src, dst, send, recv, **where):
    return pltpu.make_async_remote_copy(
        src_ref=src,
        dst_ref=dst,
        send_sem=send,
        recv_sem=recv,
        device_id=where,
        device_id_type=MESH,
    )


def loop(low, high, body):
    lax.fori_loop(low, high, lambda i, c: (body(i), c)[1], 0)


def kernel(
    n_ctx,
    n_exp,
    side,
    qkv_hbm,
    taps_hbm,
    lgate_hbm,
    beta_hbm,
    z_hbm,
    gain_hbm,
    ow_hbm,
    res_hbm,
    post_hbm,
    ids_hbm,
    rw_hbm,
    wg_ref,
    wu_ref,
    wd_ref,
    out_ref,
    qkv_ref,
    taps_ref,
    lgate_ref,
    beta_ref,
    z_ref,
    gain_ref,
    ow_ref,
    res_ref,
    post_ref,
    ids_ref,
    rw_ref,
    halo,
    xs,
    keys,
    queries,
    decays,
    solved,
    ab_send,
    ab_recv,
    st_send,
    st_recv,
    qmap,
    lout,
    normed,
    colblk,
    wbuf,
    hidden,
    gate_full,
    up_full,
    down_full,
    outbound,
    arrived,
    answer,
    returned,
    copy_gate,
    copy_up,
    copy_down,
    row_gate,
    row_down,
    col_up,
    col_down,
    load_s,
    own_s,
    zx_s,
    zx_r,
    halo_s,
    halo_r,
    col_s,
    col_r,
    band1_s,
    band1_r,
    band2_s,
    band2_r,
    core_s,
    core_r,
    ab_s,
    ab_r,
    st_s,
    st_r,
    g1_s,
    g1_r,
    u1_s,
    u1_r,
    g2_s,
    g2_r,
    u2_s,
    u2_r,
    pair_s,
    pair_r,
    out_s,
    out_r,
    back_s,
    back_r,
):
    ctx, exp = lax.axis_index("ctx"), lax.axis_index("exp")
    row, col = ctx // side, ctx % side
    tokens, width = qkv_ref.shape
    heads = width // (3 * HD)
    inner = heads * HD
    model = res_ref.shape[1]
    halfm = model // 2
    lanes = ow_ref.shape[1]
    slab = ow_ref.shape[0]
    cap = outbound.shape[1] // 2
    wrows = wg_ref.shape[0]
    chip, core = exp // 2, exp % 2
    chips = n_exp // 2
    sibling = exp + 1 - 2 * core
    composer = ctx % 2 == core

    after = chips // 8
    before = chips // 2 - 1 - after
    away = 2 * after + 1
    second, odd = col % 2, row % 2
    up = 1 - 2 * ((chip + core) % 2)
    turn = 1 - 2 * (chip % 2)
    my_up = turn * (1 - 2 * odd) * (1 - 2 * second)
    my_expert = 2 * ((chip + chips - second * away * my_up) % chips) + odd
    reach = jnp.where(second == 0, before, after)
    my_block = reach * 4 + odd * 2 + second

    barrier = pltpu.get_barrier_semaphore()

    def greet(to_ctx, to_exp):
        pl.semaphore_signal(
            barrier, inc=1, device_id={"ctx": to_ctx, "exp": to_exp}, device_id_type=MESH
        )

    def beside(j):
        return (row - odd + j // 2) * side + col - second + j % 2

    corner = odd * 2 + second
    loop(1, n_ctx, lambda d: greet((ctx + d) % n_ctx, exp))
    loop(0, n_ctx, lambda d: greet((ctx + d) % n_ctx, sibling))
    loop(1, chips, lambda d: greet(ctx, (exp + 2 * d) % n_exp))
    for j in range(4):

        @pl.when(j != corner)
        def _():
            loop(1, before + 1, lambda d: greet(beside(j), (exp + 2 * d) % n_exp))
            loop(1, before + 1, lambda d: greet(beside(j), (exp + n_exp - 2 * d) % n_exp))

    greeted = 2 * n_ctx - 1 + chips - 1 + 6 * before
    loads = [
        pltpu.make_async_copy(src, dst, load_s.at[i])
        for i, (src, dst) in enumerate(
            (
                (qkv_hbm, qkv_ref),
                (taps_hbm, taps_ref),
                (lgate_hbm, lgate_ref),
                (beta_hbm, beta_ref),
                (ow_hbm, ow_ref),
                (z_hbm, z_ref),
                (gain_hbm, gain_ref),
                (res_hbm, res_ref),
                (post_hbm, post_ref),
                (ids_hbm, ids_ref),
                (rw_hbm, rw_ref),
            )
        )
    ]
    for c in loads:
        c.start()
    half_ff = wd_ref.shape[0] // 2
    wd_first, wd_last = wd_ref.at[pl.ds(0, half_ff), :], wd_ref.at[pl.ds(half_ff, half_ff), :]
    cd_first = copy_down.at[pl.ds(0, half_ff), :]
    cd_last = copy_down.at[pl.ds(half_ff, half_ff), :]
    own_row = [
        pltpu.make_async_copy(wg_ref, row_gate.at[col], own_s.at[0]),
        pltpu.make_async_copy(wd_first, row_down.at[col], own_s.at[1]),
    ]
    own_col = [
        pltpu.make_async_copy(wu_ref, col_up.at[0, row], own_s.at[2]),
        pltpu.make_async_copy(wd_last, col_down.at[0, row], own_s.at[3]),
    ]

    @pl.when(second == 0)
    def _():
        for c in own_row:
            c.start()

    @pl.when(odd == core)
    def _():
        for c in own_col:
            c.start()

    for c in loads[:5]:
        c.wait()
    xs[8:, :] = qkv_ref[...].astype(F32)
    pl.semaphore_wait(barrier, greeted)

    halo_copy = copy_to(
        qkv_ref.at[pl.ds(tokens - HALO, HALO), :],
        halo,
        halo_s.at[0],
        halo_r.at[0],
        ctx=(ctx + 1) % n_ctx,
    )
    halo_copy.start()

    def col_copy(d):
        return copy_to(
            ow_ref, colblk.at[chip], col_s.at[d], col_r.at[d], exp=(exp + 2 * d) % n_exp
        )

    loop(1, chips, lambda d: col_copy(d).start())
    colblk[chip] = ow_ref[...]

    def along_x(d):
        return row * side + (col + d) % side

    def along_y(d):
        return ((row + d) % side) * side + col

    away_exp = 2 * ((chip + chips + away * up) % chips) + core
    zx_copies = [
        copy_to(src, dst, zx_s.at[i], zx_r.at[i], exp=away_exp)
        for i, (src, dst) in enumerate(
            ((wg_ref, copy_gate), (wu_ref, copy_up), (wd_ref, copy_down))
        )
    ]

    def unless(skip, body):
        def step(i):
            @pl.when(i != skip)
            def _():
                body(i)

        return step

    def g1_copies(kind, to):
        gate, down = ((wg_ref, wd_first), (copy_gate, cd_first))[kind]
        there = row * side + to
        return (
            copy_to(gate, row_gate.at[col], g1_s.at[0, to], g1_r.at[0, col], ctx=there),
            copy_to(down, row_down.at[col], g1_s.at[1, to], g1_r.at[1, col], ctx=there),
        )

    def g1_arrivals(src):
        there = row * side + src
        return (
            copy_to(wg_ref, row_gate.at[src], g1_s.at[0, src], g1_r.at[0, src], ctx=there),
            copy_to(wd_first, row_down.at[src], g1_s.at[1, src], g1_r.at[1, src], ctx=there),
        )

    def u1_copies(kind, j):
        up_src, down = ((wu_ref, wd_last), (copy_up, cd_last))[kind]
        there = (core + 2 * j) * side + col
        return (
            copy_to(
                up_src, col_up.at[kind, row], u1_s.at[0, kind, j], u1_r.at[0, kind, row], ctx=there
            ),
            copy_to(
                down, col_down.at[kind, row], u1_s.at[1, kind, j], u1_r.at[1, kind, row], ctx=there
            ),
        )

    def u1_arrivals(kind, src):
        there = src * side + col
        return (
            copy_to(
                wu_ref, col_up.at[kind, src], u1_s.at[0, kind, 0], u1_r.at[0, kind, src], ctx=there
            ),
            copy_to(
                wd_last,
                col_down.at[kind, src],
                u1_s.at[1, kind, 0],
                u1_r.at[1, kind, src],
                ctx=there,
            ),
        )

    halves = side // 2
    row_own = jnp.where(odd == core, row // 2, halves)

    def start_all(copies):
        for c in copies:
            c.start()

    def wait_sent(copies):
        for c in copies:
            c.wait_send()

    def wait_came(copies):
        for c in copies:
            c.wait_recv()

    def each_first(kind, act):
        for j in range(halves):
            to = 2 * j + kind

            @pl.when(to != col)
            def _():
                act(g1_copies(kind, to))

            @pl.when(j != row_own)
            def _():
                act(u1_copies(kind, j))

    start_all(zx_copies)
    each_first(0, start_all)

    tri_r = lax.broadcasted_iota(jnp.int32, (tokens, tokens), 0)
    tri_c = lax.broadcasted_iota(jnp.int32, (tokens, tokens), 1)
    causal = tri_r >= tri_c
    strict = tri_r > tri_c
    eye = (tri_r == tri_c).astype(F32)
    growth_row = lax.dot_general(
        lgate_ref[...],
        (tri_r <= tri_c).astype(F32),
        (NN, ((), ())),
        preferred_element_type=F32,
        precision=lax.Precision.HIGHEST,
    )

    def column(line):
        return jnp.sum(line * eye, axis=1, keepdims=True)

    growth = [growth_row[h : h + 1, :] for h in range(heads)]
    growth_col = [column(g) for g in growth]
    last = [g[:, tokens - 1 :] for g in growth]
    strength = [column(beta_ref[h : h + 1, :]) for h in range(heads)]
    halo_copy.wait()
    xs[:8, :] = jnp.where(ctx > 0, halo[...].astype(F32)[HALO - 8 :, :], 0.0)
    taps = taps_ref[...].astype(F32)

    def active(block):
        at = slice(block * HD, (block + 1) * HD)
        total = xs[5 : 5 + tokens, at] * taps[0:1, at]
        for j in range(1, 4):
            total = total + xs[5 + j : 5 + j + tokens, at] * taps[j : j + 1, at]
        return silu(total)

    def unit(rows):
        return rows * lax.rsqrt(jnp.sum(rows * rows, axis=-1, keepdims=True) + EPS)

    lowers = []
    for h in range(heads):
        q = unit(active(h)) * HD ** (-0.5)
        k = unit(active(heads + h))
        queries[h] = q
        keys[h] = k
        gc, gr = growth_col[h], growth[h]
        decay = jnp.where(causal, jnp.exp(jnp.where(causal, gc - gr, 0.0)), 0.0)
        decays[h] = decay
        kk = dot(k, k, NT)
        lowers.append(jnp.where(strict, strength[h] * decay * kk, 0.0))

    def col_wait(d):
        c = col_copy(d)
        c.wait_send()
        c.wait_recv()

    loop(1, chips, col_wait)
    fore, rear = pl.ds(0, chips // 2), pl.ds(chips // 2, chips // 2)

    def band1_copies(d):
        return (
            copy_to(
                colblk.at[fore],
                wbuf.at[row, col, fore, core],
                band1_s.at[0, d],
                band1_r.at[0, d],
                ctx=along_x(d),
            ),
            copy_to(
                colblk.at[rear],
                wbuf.at[row, col, rear, core],
                band1_s.at[1, d],
                band1_r.at[1, d],
                ctx=along_y(d),
            ),
        )

    def band2_copies(d):
        ahead, behind = wbuf.at[row, :, fore, core], wbuf.at[:, col, rear, core]
        return (
            copy_to(ahead, ahead, band2_s.at[0, d], band2_r.at[0, d], ctx=along_y(d)),
            copy_to(behind, behind, band2_s.at[1, d], band2_r.at[1, d], ctx=along_x(d)),
        )

    for d in range(1, side):
        for c in band1_copies(d):
            c.start()
    wbuf[row, col, :, core] = colblk[...]

    def same(size):
        return tri_r // size == tri_c // size

    base = 16
    near = same(base)
    power = [jnp.where(near, l, 0.0) for l in lowers]
    inv = [eye - p for p in power]
    for _ in range(3):
        power = [dot(p, p) for p in power]
        inv = [x + dot(x, p) for x, p in zip(inv, power)]
    size = base
    while size < tokens:
        ring = jnp.logical_and(same(2 * size), jnp.logical_not(same(size)))
        mid = [dot(jnp.where(ring, l, 0.0), x) for l, x in zip(lowers, inv)]
        inv = [x - dot(x, m) for x, m in zip(inv, mid)]
        size *= 2

    def ab_copy(h):
        to = 2 * h + core
        return copy_to(ab_send.at[h], ab_recv.at[ctx], ab_s.at[h], ab_r.at[ctx], ctx=to)

    def ab_arrival(src):
        return copy_to(ab_send.at[0], ab_recv.at[src], ab_s.at[0], ab_r.at[src], ctx=src)

    mine = jnp.where(composer, ctx // 2, n_ctx)
    for h in range(heads):
        b = strength[h]
        gc = growth_col[h]
        k = keys[h]
        v = active(2 * heads + h)
        rhs = jnp.concatenate([(b * jnp.exp(gc)) * k, b * v], axis=1)
        sol = dot(inv[h], rhs).astype(BF16)
        solved[h] = sol
        kept = jnp.exp(last[h] - gc) * k
        both = dot(sol, kept, TN)
        at = (jnp.exp(last[h]) * eye - both[:HD, :]).astype(BF16)
        bt = both[HD:, :].astype(BF16)
        ab_send[h, :HD, :] = at
        ab_send[h, HD:, :] = bt

        @pl.when(h != mine)
        def _():
            ab_copy(h).start()

    @pl.when(composer)
    def _():
        ab_recv[ctx] = ab_send[ctx // 2]


    for d in range(1, side):
        for c in band1_copies(d):
            c.wait_send()
            c.wait_recv()
    for d in range(1, side):
        for c in band2_copies(d):
            c.start()

    def core_copies(d):
        r, q = (row + side - d) % side, (col + side - d) % side
        ahead, behind = wbuf.at[r, :, fore, core], wbuf.at[:, q, rear, core]
        return (
            copy_to(ahead, ahead, core_s.at[0, d], core_r.at[0, d], exp=sibling),
            copy_to(behind, behind, core_s.at[1, d], core_r.at[1, d], exp=sibling),
        )

    for c in core_copies(0):
        c.start()

    for h in range(heads):
        gc = growth_col[h]
        q = queries[h]
        qk = decays[h] * dot(q, keys[h], NT)
        both = dot(qk, solved[h])
        qmap[h] = (jnp.exp(gc) * q - both[:, :HD]).astype(BF16)
        lout[h] = both[:, HD:]

    def st_copy(to):
        return copy_to(
            st_send.at[to], st_recv.at[ctx // 2], st_s.at[to], st_r.at[ctx // 2], ctx=to
        )

    @pl.when(composer)
    def _():
        loop(0, n_ctx, unless(ctx, lambda src: ab_arrival(src).wait_recv()))
        state = jnp.zeros((HD, HD), F32)
        for c in range(n_ctx):
            high = state.astype(BF16)
            st_send[c] = high

            @pl.when(ctx != c)
            def _():
                st_copy(c).start()

            if c < n_ctx - 1:
                low = (state - high.astype(F32)).astype(BF16)
                parts = dot(jnp.concatenate([high, low], axis=0), ab_recv[c, :HD, :])
                state = parts[:HD] + parts[HD:] + ab_recv[c, HD:, :].astype(F32)
        st_recv[ctx // 2] = st_send[ctx]

    for c in zx_copies:
        c.wait_recv()
    each_first(1, start_all)

    @pl.when(second == 0)
    def _():
        for c in own_row:
            c.wait()

    @pl.when(second == 1)
    def _():
        row_gate[col] = copy_gate[...]
        row_down[col] = copy_down[:half_ff, :]

    @pl.when(odd == core)
    def _():
        for c in own_col:
            c.wait()
        col_up[1, row] = copy_up[...]
        col_down[1, row] = copy_down[half_ff:, :]

    for d in range(1, side):
        for c, onward in zip(band2_copies(d), core_copies(d)):
            c.wait_send()
            c.wait_recv()
            onward.start()

    def st_arrival(h):
        src = 2 * h + core
        return copy_to(st_send.at[0], st_recv.at[h], st_s.at[0], st_r.at[h], ctx=src)

    loop(0, heads, unless(mine, lambda h: st_arrival(h).wait_recv()))
    loop(0, heads, unless(mine, lambda h: ab_copy(h).wait_send()))

    @pl.when(composer)
    def _():
        loop(0, n_ctx, unless(ctx, lambda to: st_copy(to).wait_send()))

    def g2_copies(j):
        there = (core + 2 * j) * side + col
        return (
            copy_to(
                row_gate, gate_full.at[row], g2_s.at[0, j], g2_r.at[0, row], ctx=there, exp=2 * chip
            ),
            copy_to(
                row_down,
                down_full.at[0, row],
                g2_s.at[1, j],
                g2_r.at[1, row],
                ctx=there,
                exp=2 * chip,
            ),
        )

    def g2_arrivals(src):
        there = src * side + col
        return (
            copy_to(
                row_gate,
                gate_full.at[src],
                g2_s.at[0, 0],
                g2_r.at[0, src],
                ctx=there,
                exp=2 * chip + odd,
            ),
            copy_to(
                row_down,
                down_full.at[0, src],
                g2_s.at[1, 0],
                g2_r.at[1, src],
                ctx=there,
                exp=2 * chip + odd,
            ),
        )

    def u2_copies(kind, j):
        there = row * side + 2 * j + kind
        return (
            copy_to(
                col_up.at[kind],
                up_full.at[:, col],
                u2_s.at[0, kind, j],
                u2_r.at[0, col],
                ctx=there,
                exp=2 * chip + 1,
            ),
            copy_to(
                col_down.at[kind],
                down_full.at[1, :, col],
                u2_s.at[1, kind, j],
                u2_r.at[1, col],
                ctx=there,
                exp=2 * chip + 1,
            ),
        )

    def u2_arrivals(src):
        there = row * side + src
        return (
            copy_to(
                col_up.at[0],
                up_full.at[:, src],
                u2_s.at[0, 0, 0],
                u2_r.at[0, src],
                ctx=there,
                exp=2 * chip + odd,
            ),
            copy_to(
                col_down.at[0],
                down_full.at[1, :, src],
                u2_s.at[1, 0, 0],
                u2_r.at[1, src],
                ctx=there,
                exp=2 * chip + odd,
            ),
        )

    g2_own = jnp.where(jnp.logical_and(core == 0, odd == 0), row // 2, halves)
    u2_own = jnp.where(jnp.logical_and(core == 1, odd == 1), col, side)

    def each_second(act):
        for j in range(halves):

            @pl.when(j != g2_own)
            def _():
                act(g2_copies(j))

        @pl.when(odd == core)
        def _():
            for kind in range(2):
                for j in range(halves):

                    @pl.when(2 * j + kind != u2_own)
                    def _():
                        act(u2_copies(kind, j))

    loop(0, side, unless(col, lambda src: wait_came(g1_arrivals(src))))

    @pl.when(odd == core)
    def _():
        for kind in range(2):
            loop(0, side, unless(row, lambda src: wait_came(u1_arrivals(kind, src))))

    each_second(start_all)

    @pl.when(g2_own < halves)
    def _():
        gate_full[row] = row_gate[...]
        down_full[0, row] = row_down[...]

    @pl.when(u2_own < side)
    def _():
        for r in range(side):
            up_full[r, col] = col_up[second, r]
            down_full[1, r, col] = col_down[second, r]

    for c in loads[5:]:
        c.wait()
    gain = gain_ref[...]
    for h in range(heads):
        read = dot(qmap[h], st_recv[h], NT) + lout[h]
        scale = lax.rsqrt(jnp.mean(read * read, axis=-1, keepdims=True) + EPS)
        z = z_ref[:, h * HD : (h + 1) * HD].astype(F32)
        normed[:, h * HD : (h + 1) * HD] = (read * scale * gain * silu(z)).astype(BF16)

    for d in range(side):
        for c in core_copies(d):
            c.wait_send()
            c.wait_recv()

    squares = jnp.zeros((tokens, 1), F32)
    act = normed[...]
    for j in range(n_ctx):
        at = slice(j * lanes, (j + 1) * lanes)
        hid = (res_ref[:, at].astype(F32) + dot(act, wbuf[j // side, j % side].reshape(inner, lanes))).astype(BF16)
        hidden[:, at] = hid
        hid = hid.astype(F32)
        squares = squares + jnp.sum(hid * hid, axis=-1, keepdims=True)
    scale = lax.rsqrt(squares / model + EPS)
    routed_in = (hidden[...].astype(F32) * scale * post_ref[...]).astype(BF16)

    ids = column(ids_ref[...].astype(F32)).astype(jnp.int32)
    member = lax.broadcasted_iota(jnp.int32, (tokens, n_exp), 1) == ids
    member = member.astype(F32)
    ranks = dot(causal.astype(F32), member)
    slot = jnp.sum(ranks * member, axis=1, keepdims=True).astype(jnp.int32) - 1
    first = ids * (2 * cap) + slot
    places = lax.broadcasted_iota(jnp.int32, (tokens, 2 * cap * n_exp), 1)
    pick_low = (places == first).astype(F32).astype(BF16)
    pick_high = (places == first + cap).astype(F32).astype(BF16)
    sent = dot(pick_low, routed_in[:, :halfm], TN) + dot(pick_high, routed_in[:, halfm:], TN)
    outbound[...] = sent.astype(BF16).reshape(outbound.shape)

    def out_copy(k, c):
        rise = 1 - 2 * ((k + c) % 2)
        place = (-k * rise) % chips
        spread = (place + before) % chips
        if spread < chips // 2:
            kind, shift = 0, k % chips
        else:
            kind, shift, spread = 1, (k + away * rise) % chips, spread - chips // 2
        to_ctx = (row - odd + c) * side + col - second + kind
        to_exp = (exp + 2 * turn * shift + 2 * n_exp) % n_exp
        block = spread * 4 + odd * 2 + second
        what = copy_to(
            outbound.at[(2 * chip + 2 * turn * k + 2 * n_exp) % n_exp + c],
            arrived.at[block],
            out_s.at[2 * k + c],
            out_r.at[block],
            ctx=to_ctx,
            exp=to_exp,
        )
        if shift:
            return what, None
        return what, jnp.logical_and(odd == c, second == kind)

    def each_out(act):
        for k in range(chips):
            for c in range(2):
                what, here = out_copy(k, c)
                if here is None:
                    act([what])
                else:

                    @pl.when(jnp.logical_not(here))
                    def _():
                        act([what])

    each_out(start_all)
    arrived[my_block] = outbound[my_expert]

    def pair_copies(i, which):
        parts = (
            (gate_full.at[i], down_full.at[0, i]),
            (up_full.at[:, i], down_full.at[1, :, i]),
        )[which]
        return [
            copy_to(
                part, part, pair_s.at[2 * which + n, i], pair_r.at[2 * which + n, i], exp=sibling
            )
            for n, part in enumerate(parts)
        ]

    @pl.when(core == 0)
    def _():
        def onward(src):
            @pl.when(jnp.logical_or(src != row, odd == 1))
            def _():
                wait_came(g2_arrivals(src))

            start_all(pair_copies(src, 0))

        loop(0, side, onward)

    @pl.when(core == 1)
    def _():
        def onward(src):
            @pl.when(jnp.logical_or(src != col, odd == 0))
            def _():
                wait_came(u2_arrivals(src))

            start_all(pair_copies(src, 1))

        loop(0, side, onward)

    wait_sent(zx_copies)
    each_first(0, wait_sent)
    each_first(1, wait_sent)
    each_second(wait_sent)

    @pl.when(core == 0)
    def _():
        for i in range(side):
            wait_sent(pair_copies(i, 0))
            wait_came(pair_copies(i, 1))

    @pl.when(core == 1)
    def _():
        for i in range(side):
            wait_sent(pair_copies(i, 1))
            wait_came(pair_copies(i, 0))

    def out_arrival(block):
        return copy_to(
            outbound.at[0], arrived.at[block], out_s.at[0], out_r.at[block], exp=sibling
        )

    loop(0, n_exp, unless(my_block, lambda block: out_arrival(block).wait_recv()))
    each_out(wait_sent)

    ff = wg_ref.shape[1]
    came = arrived[...].astype(F32)
    rows_in = jnp.concatenate(
        [
            came[:, :cap, :].reshape(n_exp * cap, halfm),
            came[:, cap:, :].reshape(n_exp * cap, halfm),
        ],
        axis=1,
    ).astype(BF16)
    gate_part = dot(rows_in, gate_full[...].reshape(model, ff))
    up_part = dot(rows_in, up_full[...].reshape(model, ff))
    activated = (silu(gate_part) * up_part).astype(BF16)
    blocks = n_ctx // 2
    for j in range(blocks):
        parts = []
        for i in (j, j + blocks):
            down = jnp.concatenate(
                [down_full[0, i // side, i % side], down_full[1, i // side, i % side]], axis=0
            )
            parts.append(dot(activated, down).reshape(n_exp, cap, lanes))
        answer[:, :, j * lanes : (j + 1) * lanes] = jnp.concatenate(parts, axis=1).astype(BF16)

    def back_copy(block):
        far = (block // 4 + chips - reach) * my_up + 2 * chips
        return copy_to(
            answer.at[block],
            returned.at[my_expert],
            back_s.at[block],
            back_r.at[my_expert],
            ctx=beside(block % 4),
            exp=2 * ((chip + far) % chips) + core,
        )

    def back_arrival(expert):
        return copy_to(
            answer.at[0], returned.at[expert], back_s.at[0], back_r.at[expert], exp=sibling
        )

    loop(0, n_exp, unless(my_block, lambda block: back_copy(block).start()))
    returned[my_expert] = answer[my_block]
    loop(0, n_exp, unless(my_expert, lambda expert: back_arrival(expert).wait_recv()))
    loop(0, n_exp, unless(my_block, lambda block: back_copy(block).wait_send()))

    back = returned[...].reshape(2 * cap * n_exp, halfm)
    weight = column(rw_ref[...])
    for pick, at in ((pick_low, slice(0, halfm)), (pick_high, slice(halfm, model))):
        fetched = dot(pick, back)
        out_ref[:, at] = (hidden[:, at].astype(F32) + weight * fetched).astype(BF16)


def on_device(n_ctx, n_exp, *args):
    (qkv, taps, lgate, beta, z, gain, ow, res, post, ids, rw, wg, wu, wd) = args
    tokens, width = qkv.shape[1:]
    heads = lgate.shape[2]
    model = res.shape[2]
    ff = wg.shape[2]
    side = math.isqrt(n_ctx)
    cap = 2 * ids.shape[2] * tokens // n_exp
    inner = heads * HD
    lanes = ow.shape[1]
    chips = n_exp // 2
    sem = pltpu.SemaphoreType.DMA
    operands = (
        qkv[0],
        taps,
        lgate[0].T,
        beta[0].T,
        z[0],
        gain[None],
        ow,
        res[0],
        post[None],
        ids[0].T,
        rw[0].T,
        wg[0],
        wu[0],
        wd[0],
    )
    slots = (n_exp, 2 * cap, model // 2)
    scratch = [pltpu.VMEM(x.shape, x.dtype) for x in operands[:11]]
    scratch += [
        pltpu.VMEM((HALO, width), BF16),
        pltpu.VMEM((8 + tokens, width), F32),
        pltpu.VMEM((heads, tokens, HD), F32),
        pltpu.VMEM((heads, tokens, HD), F32),
        pltpu.VMEM((heads, tokens, tokens), F32),
        pltpu.VMEM((heads, tokens, 2 * HD), BF16),
        pltpu.VMEM((heads, 2 * HD, HD), BF16),
        pltpu.VMEM((n_ctx, 2 * HD, HD), BF16),
        pltpu.VMEM((n_ctx, HD, HD), BF16),
        pltpu.VMEM((heads, HD, HD), BF16),
        pltpu.VMEM((heads, tokens, HD), BF16),
        pltpu.VMEM((heads, tokens, HD), F32),
        pltpu.VMEM((tokens, inner), BF16),
        pltpu.VMEM((chips, ow.shape[0], lanes), BF16),
        pltpu.VMEM((side, side, chips, 2, ow.shape[0], lanes), BF16),
        pltpu.VMEM((tokens, model), BF16),
        pltpu.VMEM((side, side, model // n_ctx, ff), BF16),
        pltpu.VMEM((side, side, model // n_ctx, ff), BF16),
        pltpu.VMEM((2, side, side, ff // 2, lanes), BF16),
        pltpu.VMEM(slots, BF16),
        pltpu.VMEM(slots, BF16),
        pltpu.VMEM(slots, BF16),
        pltpu.VMEM(slots, BF16),
        pltpu.VMEM((model // n_ctx, ff), BF16),
        pltpu.VMEM((model // n_ctx, ff), BF16),
        pltpu.VMEM((ff, lanes), BF16),
        pltpu.VMEM((side, model // n_ctx, ff), BF16),
        pltpu.VMEM((side, ff // 2, lanes), BF16),
        pltpu.VMEM((2, side, model // n_ctx, ff), BF16),
        pltpu.VMEM((2, side, ff // 2, lanes), BF16),
        sem((11,)),
        sem((4,)),
        sem((3,)),
        sem((3,)),
        sem((1,)),
        sem((1,)),
        sem((chips,)),
        sem((chips,)),
        sem((2, side)),
        sem((2, side)),
        sem((2, side)),
        sem((2, side)),
        sem((2, side)),
        sem((2, side)),
        sem((heads,)),
        sem((n_ctx,)),
        sem((n_ctx,)),
        sem((heads,)),
        sem((2, side)),
        sem((2, side)),
        sem((2, 2, side)),
        sem((2, 2, side)),
        sem((2, side)),
        sem((2, side)),
        sem((2, 2, side)),
        sem((2, side)),
        sem((4, side)),
        sem((4, side)),
        sem((n_exp,)),
        sem((n_exp,)),
        sem((n_exp,)),
        sem((n_exp,)),
    ]
    out = pl.pallas_call(
        functools.partial(kernel, n_ctx, n_exp, side),
        out_shape=jax.ShapeDtypeStruct((tokens, model), BF16),
        in_specs=[pl.BlockSpec(memory_space=pltpu.HBM)] * 14,
        out_specs=pl.BlockSpec(memory_space=pltpu.VMEM),
        scratch_shapes=scratch,
        compiler_params=pltpu.CompilerParams(
            collective_id=0, has_side_effects=True, vmem_limit_bytes=63 * 2**20
        ),
    )(*operands)
    return out[None]


def solution(mesh):
    placed = (
        P("exp", "ctx", None),
        P(),
        P("exp", "ctx", None),
        P("exp", "ctx", None),
        P("exp", "ctx", None),
        P(),
        P("exp", "ctx"),
        P("exp", "ctx", None),
        P(),
        P("exp", "ctx", None),
        P("exp", "ctx", None),
        P("exp", "ctx", None),
        P("exp", "ctx", None),
        P("exp", None, "ctx"),
    )
    return jax.shard_map(
        functools.partial(on_device, mesh.shape["ctx"], mesh.shape["exp"]),
        mesh=mesh,
        in_specs=placed,
        out_specs=P("exp", "ctx", None),
        check_vma=False,
    )
```

```python
import functools
import math

import jax
import jax.numpy as jnp
from jax import lax
from jax.experimental import pallas as pl
from jax.experimental.pallas import tpu as pltpu
from jax.sharding import PartitionSpec as P

MESH = pl.DeviceIdType.MESH
F32, BF16 = jnp.float32, jnp.bfloat16
NN, NT, TN = ((1,), (0,)), ((1,), (1,)), ((0,), (0,))
EPS = 1e-06
HD = 128
HALO = 16


def dot(a, b, dims=NN):
    return lax.dot_general(
        a.astype(BF16), b.astype(BF16), (dims, ((), ())), preferred_element_type=F32
    )


def silu(u):
    return u / (1.0 + jnp.exp(-u))


def copy_to(src, dst, send, recv, **where):
    return pltpu.make_async_remote_copy(
        src_ref=src,
        dst_ref=dst,
        send_sem=send,
        recv_sem=recv,
        device_id=where,
        device_id_type=MESH,
    )


def loop(low, high, body):
    lax.fori_loop(low, high, lambda i, c: (body(i), c)[1], 0)


def kernel(
    n_ctx,
    n_exp,
    side,
    qkv_hbm,
    taps_hbm,
    lgate_hbm,
    beta_hbm,
    z_hbm,
    gain_hbm,
    ow_hbm,
    res_hbm,
    post_hbm,
    ids_hbm,
    rw_hbm,
    wg_ref,
    wu_ref,
    wd_ref,
    out_ref,
    qkv_ref,
    taps_ref,
    lgate_ref,
    beta_ref,
    z_ref,
    gain_ref,
    ow_ref,
    res_ref,
    post_ref,
    ids_ref,
    rw_ref,
    halo,
    xs,
    keys,
    queries,
    decays,
    solved,
    ab_send,
    ab_recv,
    st_send,
    st_recv,
    qmap,
    lout,
    normed,
    colblk,
    wbuf,
    hidden,
    gate_full,
    up_full,
    down_full,
    outbound,
    arrived,
    answer,
    returned,
    copy_gate,
    copy_up,
    copy_down,
    row_gate,
    row_down,
    col_up,
    col_down,
    load_s,
    own_s,
    zx_s,
    zx_r,
    halo_s,
    halo_r,
    col_s,
    col_r,
    band1_s,
    band1_r,
    band2_s,
    band2_r,
    core_s,
    core_r,
    ab_s,
    ab_r,
    st_s,
    st_r,
    g1_s,
    g1_r,
    u1_s,
    u1_r,
    g2_s,
    g2_r,
    u2_s,
    u2_r,
    pair_s,
    pair_r,
    out_s,
    out_r,
    back_s,
    back_r,
):
    ctx, exp = lax.axis_index("ctx"), lax.axis_index("exp")
    row, col = ctx // side, ctx % side
    tokens, width = qkv_ref.shape
    heads = width // (3 * HD)
    inner = heads * HD
    model = res_ref.shape[1]
    halfm = model // 2
    lanes = ow_ref.shape[1]
    slab = ow_ref.shape[0]
    cap = outbound.shape[1] // 2
    wrows = wg_ref.shape[0]
    chip, core = exp // 2, exp % 2
    chips = n_exp // 2
    sibling = exp + 1 - 2 * core
    composer = ctx % 2 == core

    after = chips // 8
    before = chips // 2 - 1 - after
    away = 2 * after + 1
    second, odd = col % 2, row % 2
    up = 1 - 2 * ((chip + core) % 2)
    turn = 1 - 2 * (chip % 2)
    my_up = turn * (1 - 2 * odd) * (1 - 2 * second)
    my_expert = 2 * ((chip + chips - second * away * my_up) % chips) + odd
    reach = jnp.where(second == 0, before, after)
    my_block = reach * 4 + odd * 2 + second

    barrier = pltpu.get_barrier_semaphore()

    def greet(to_ctx, to_exp):
        pl.semaphore_signal(
            barrier, inc=1, device_id={"ctx": to_ctx, "exp": to_exp}, device_id_type=MESH
        )

    def beside(j):
        return (row - odd + j // 2) * side + col - second + j % 2

    corner = odd * 2 + second
    loop(1, n_ctx, lambda d: greet((ctx + d) % n_ctx, exp))
    loop(0, n_ctx, lambda d: greet((ctx + d) % n_ctx, sibling))
    loop(1, chips, lambda d: greet(ctx, (exp + 2 * d) % n_exp))
    for j in range(4):

        @pl.when(j != corner)
        def _():
            loop(1, before + 1, lambda d: greet(beside(j), (exp + 2 * d) % n_exp))
            loop(1, before + 1, lambda d: greet(beside(j), (exp + n_exp - 2 * d) % n_exp))

    greeted = 2 * n_ctx - 1 + chips - 1 + 6 * before
    loads = [
        pltpu.make_async_copy(src, dst, load_s.at[i])
        for i, (src, dst) in enumerate(
            (
                (qkv_hbm, qkv_ref),
                (taps_hbm, taps_ref),
                (lgate_hbm, lgate_ref),
                (beta_hbm, beta_ref),
                (ow_hbm, ow_ref),
                (z_hbm, z_ref),
                (gain_hbm, gain_ref),
                (res_hbm, res_ref),
                (post_hbm, post_ref),
                (ids_hbm, ids_ref),
                (rw_hbm, rw_ref),
            )
        )
    ]
    for c in loads:
        c.start()
    half_ff = wd_ref.shape[0] // 2
    wd_first, wd_last = wd_ref.at[pl.ds(0, half_ff), :], wd_ref.at[pl.ds(half_ff, half_ff), :]
    cd_first = copy_down.at[pl.ds(0, half_ff), :]
    cd_last = copy_down.at[pl.ds(half_ff, half_ff), :]
    own_row = [
        pltpu.make_async_copy(wg_ref, row_gate.at[col], own_s.at[0]),
        pltpu.make_async_copy(wd_first, row_down.at[col], own_s.at[1]),
    ]
    own_col = [
        pltpu.make_async_copy(wu_ref, col_up.at[0, row], own_s.at[2]),
        pltpu.make_async_copy(wd_last, col_down.at[0, row], own_s.at[3]),
    ]

    @pl.when(second == 0)
    def _():
        for c in own_row:
            c.start()

    @pl.when(odd == core)
    def _():
        for c in own_col:
            c.start()

    for c in loads[:5]:
        c.wait()
    xs[8:, :] = qkv_ref[...].astype(F32)
    pl.semaphore_wait(barrier, greeted)

    halo_copy = copy_to(
        qkv_ref.at[pl.ds(tokens - HALO, HALO), :],
        halo,
        halo_s.at[0],
        halo_r.at[0],
        ctx=(ctx + 1) % n_ctx,
    )
    halo_copy.start()

    def col_copy(d):
        return copy_to(
            ow_ref, colblk.at[chip], col_s.at[d], col_r.at[d], exp=(exp + 2 * d) % n_exp
        )

    loop(1, chips, lambda d: col_copy(d).start())
    colblk[chip] = ow_ref[...]

    def along_x(d):
        return row * side + (col + d) % side

    def along_y(d):
        return ((row + d) % side) * side + col

    away_exp = 2 * ((chip + chips + away * up) % chips) + core
    zx_copies = [
        copy_to(src, dst, zx_s.at[i], zx_r.at[i], exp=away_exp)
        for i, (src, dst) in enumerate(
            ((wg_ref, copy_gate), (wu_ref, copy_up), (wd_ref, copy_down))
        )
    ]

    def unless(skip, body):
        def step(i):
            @pl.when(i != skip)
            def _():
                body(i)

        return step

    def g1_copies(kind, to):
        gate, down = ((wg_ref, wd_first), (copy_gate, cd_first))[kind]
        there = row * side + to
        return (
            copy_to(gate, row_gate.at[col], g1_s.at[0, to], g1_r.at[0, col], ctx=there),
            copy_to(down, row_down.at[col], g1_s.at[1, to], g1_r.at[1, col], ctx=there),
        )

    def g1_arrivals(src):
        there = row * side + src
        return (
            copy_to(wg_ref, row_gate.at[src], g1_s.at[0, src], g1_r.at[0, src], ctx=there),
            copy_to(wd_first, row_down.at[src], g1_s.at[1, src], g1_r.at[1, src], ctx=there),
        )

    def u1_copies(kind, j):
        up_src, down = ((wu_ref, wd_last), (copy_up, cd_last))[kind]
        there = (core + 2 * j) * side + col
        return (
            copy_to(
                up_src, col_up.at[kind, row], u1_s.at[0, kind, j], u1_r.at[0, kind, row], ctx=there
            ),
            copy_to(
                down, col_down.at[kind, row], u1_s.at[1, kind, j], u1_r.at[1, kind, row], ctx=there
            ),
        )

    def u1_arrivals(kind, src):
        there = src * side + col
        return (
            copy_to(
                wu_ref, col_up.at[kind, src], u1_s.at[0, kind, 0], u1_r.at[0, kind, src], ctx=there
            ),
            copy_to(
                wd_last,
                col_down.at[kind, src],
                u1_s.at[1, kind, 0],
                u1_r.at[1, kind, src],
                ctx=there,
            ),
        )

    halves = side // 2
    row_own = jnp.where(odd == core, row // 2, halves)

    def start_all(copies):
        for c in copies:
            c.start()

    def wait_sent(copies):
        for c in copies:
            c.wait_send()

    def wait_came(copies):
        for c in copies:
            c.wait_recv()

    def each_first(kind, act):
        for j in range(halves):
            to = 2 * j + kind

            @pl.when(to != col)
            def _():
                act(g1_copies(kind, to))

            @pl.when(j != row_own)
            def _():
                act(u1_copies(kind, j))

    each_first(0, start_all)

    tri_r = lax.broadcasted_iota(jnp.int32, (tokens, tokens), 0)
    tri_c = lax.broadcasted_iota(jnp.int32, (tokens, tokens), 1)
    causal = tri_r >= tri_c
    strict = tri_r > tri_c
    eye = (tri_r == tri_c).astype(F32)
    growth_row = lax.dot_general(
        lgate_ref[...],
        (tri_r <= tri_c).astype(F32),
        (NN, ((), ())),
        preferred_element_type=F32,
        precision=lax.Precision.HIGHEST,
    )

    def column(line):
        return jnp.sum(line * eye, axis=1, keepdims=True)

    growth = [growth_row[h : h + 1, :] for h in range(heads)]
    growth_col = [column(g) for g in growth]
    last = [g[:, tokens - 1 :] for g in growth]
    strength = [column(beta_ref[h : h + 1, :]) for h in range(heads)]
    halo_copy.wait_recv()
    xs[:8, :] = jnp.where(ctx > 0, halo[...].astype(F32)[HALO - 8 :, :], 0.0)
    taps = taps_ref[...].astype(F32)

    def active(block):
        at = slice(block * HD, (block + 1) * HD)
        total = xs[5 : 5 + tokens, at] * taps[0:1, at]
        for j in range(1, 4):
            total = total + xs[5 + j : 5 + j + tokens, at] * taps[j : j + 1, at]
        return silu(total)

    def unit(rows):
        return rows * lax.rsqrt(jnp.sum(rows * rows, axis=-1, keepdims=True) + EPS)

    lowers = []
    for h in range(heads):
        q = unit(active(h)) * HD ** (-0.5)
        k = unit(active(heads + h))
        queries[h] = q
        keys[h] = k
        gc, gr = growth_col[h], growth[h]
        decay = jnp.where(causal, jnp.exp(jnp.where(causal, gc - gr, 0.0)), 0.0)
        decays[h] = decay
        kk = dot(k, k, NT)
        lowers.append(jnp.where(strict, strength[h] * decay * kk, 0.0))

    loop(1, chips, lambda d: col_copy(d).wait_recv())
    start_all(zx_copies)
    fore, rear = pl.ds(0, chips // 2), pl.ds(chips // 2, chips // 2)

    def band1_copies(d):
        return (
            copy_to(
                colblk.at[fore],
                wbuf.at[row, col, fore, core],
                band1_s.at[0, d],
                band1_r.at[0, d],
                ctx=along_x(d),
            ),
            copy_to(
                colblk.at[rear],
                wbuf.at[row, col, rear, core],
                band1_s.at[1, d],
                band1_r.at[1, d],
                ctx=along_y(d),
            ),
        )

    def band2_copies(d):
        ahead, behind = wbuf.at[row, :, fore, core], wbuf.at[:, col, rear, core]
        return (
            copy_to(ahead, ahead, band2_s.at[0, d], band2_r.at[0, d], ctx=along_y(d)),
            copy_to(behind, behind, band2_s.at[1, d], band2_r.at[1, d], ctx=along_x(d)),
        )

    for d in range(1, side):
        for c in band1_copies(d):
            c.start()
    wbuf[row, col, :, core] = colblk[...]

    def same(size):
        return tri_r // size == tri_c // size

    base = 16
    near = same(base)
    power = [jnp.where(near, l, 0.0) for l in lowers]
    inv = [eye - p for p in power]
    for _ in range(3):
        power = [dot(p, p) for p in power]
        inv = [x + dot(x, p) for x, p in zip(inv, power)]
    size = base
    while size < tokens:
        ring = jnp.logical_and(same(2 * size), jnp.logical_not(same(size)))
        mid = [dot(jnp.where(ring, l, 0.0), x) for l, x in zip(lowers, inv)]
        inv = [x - dot(x, m) for x, m in zip(inv, mid)]
        size *= 2

    def ab_copy(h):
        to = 2 * h + core
        return copy_to(ab_send.at[h], ab_recv.at[ctx], ab_s.at[h], ab_r.at[ctx], ctx=to)

    def ab_arrival(src):
        return copy_to(ab_send.at[0], ab_recv.at[src], ab_s.at[0], ab_r.at[src], ctx=src)

    mine = jnp.where(composer, ctx // 2, n_ctx)
    for h in range(heads):
        b = strength[h]
        gc = growth_col[h]
        k = keys[h]
        v = active(2 * heads + h)
        rhs = jnp.concatenate([(b * jnp.exp(gc)) * k, b * v], axis=1)
        sol = dot(inv[h], rhs).astype(BF16)
        solved[h] = sol
        kept = jnp.exp(last[h] - gc) * k
        both = dot(sol, kept, TN)
        at = (jnp.exp(last[h]) * eye - both[:HD, :]).astype(BF16)
        bt = both[HD:, :].astype(BF16)
        ab_send[h, :HD, :] = at
        ab_send[h, HD:, :] = bt

        @pl.when(h != mine)
        def _():
            ab_copy(h).start()

    @pl.when(composer)
    def _():
        ab_recv[ctx] = ab_send[ctx // 2]


    for d in range(1, side):
        wait_came(band1_copies(d))
    for d in range(1, side):
        for c in band2_copies(d):
            c.start()

    def core_copies(d):
        r, q = (row + side - d) % side, (col + side - d) % side
        ahead, behind = wbuf.at[r, :, fore, core], wbuf.at[:, q, rear, core]
        return (
            copy_to(ahead, ahead, core_s.at[0, d], core_r.at[0, d], exp=sibling),
            copy_to(behind, behind, core_s.at[1, d], core_r.at[1, d], exp=sibling),
        )

    for c in core_copies(0):
        c.start()

    for h in range(heads):
        gc = growth_col[h]
        q = queries[h]
        qk = decays[h] * dot(q, keys[h], NT)
        both = dot(qk, solved[h])
        qmap[h] = (jnp.exp(gc) * q - both[:, :HD]).astype(BF16)
        lout[h] = both[:, HD:]

    def st_copy(to):
        return copy_to(
            st_send.at[to], st_recv.at[ctx // 2], st_s.at[to], st_r.at[ctx // 2], ctx=to
        )

    @pl.when(composer)
    def _():
        loop(0, n_ctx, unless(ctx, lambda src: ab_arrival(src).wait_recv()))
        state = jnp.zeros((HD, HD), F32)
        for c in range(n_ctx):
            high = state.astype(BF16)
            st_send[c] = high

            @pl.when(ctx != c)
            def _():
                st_copy(c).start()

            if c < n_ctx - 1:
                low = (state - high.astype(F32)).astype(BF16)
                parts = dot(jnp.concatenate([high, low], axis=0), ab_recv[c, :HD, :])
                state = parts[:HD] + parts[HD:] + ab_recv[c, HD:, :].astype(F32)
        st_recv[ctx // 2] = st_send[ctx]

    for d in range(1, side):
        for c, onward in zip(band2_copies(d), core_copies(d)):
            c.wait_recv()
            onward.start()

    def st_arrival(h):
        src = 2 * h + core
        return copy_to(st_send.at[0], st_recv.at[h], st_s.at[0], st_r.at[h], ctx=src)

    loop(0, heads, unless(mine, lambda h: st_arrival(h).wait_recv()))
    for c in loads[5:]:
        c.wait()
    gain = gain_ref[...]
    for h in range(heads):
        read = dot(qmap[h], st_recv[h], NT) + lout[h]
        scale = lax.rsqrt(jnp.mean(read * read, axis=-1, keepdims=True) + EPS)
        z = z_ref[:, h * HD : (h + 1) * HD].astype(F32)
        normed[:, h * HD : (h + 1) * HD] = (read * scale * gain * silu(z)).astype(BF16)

    for c in zx_copies:
        c.wait_recv()
    each_first(1, start_all)

    @pl.when(second == 0)
    def _():
        for c in own_row:
            c.wait()

    @pl.when(second == 1)
    def _():
        row_gate[col] = copy_gate[...]
        row_down[col] = copy_down[:half_ff, :]

    @pl.when(odd == core)
    def _():
        for c in own_col:
            c.wait()
        col_up[1, row] = copy_up[...]
        col_down[1, row] = copy_down[half_ff:, :]

    for d in range(side):
        wait_came(core_copies(d))

    squares = jnp.zeros((tokens, 1), F32)
    act = normed[...]
    for j in range(n_ctx):
        at = slice(j * lanes, (j + 1) * lanes)
        hid = (res_ref[:, at].astype(F32) + dot(act, wbuf[j // side, j % side].reshape(inner, lanes))).astype(BF16)
        hidden[:, at] = hid
        hid = hid.astype(F32)
        squares = squares + jnp.sum(hid * hid, axis=-1, keepdims=True)
    scale = lax.rsqrt(squares / model + EPS)
    routed_in = (hidden[...].astype(F32) * scale * post_ref[...]).astype(BF16)

    ids = column(ids_ref[...].astype(F32)).astype(jnp.int32)
    member = lax.broadcasted_iota(jnp.int32, (tokens, n_exp), 1) == ids
    member = member.astype(F32)
    ranks = dot(causal.astype(F32), member)
    slot = jnp.sum(ranks * member, axis=1, keepdims=True).astype(jnp.int32) - 1
    first = ids * (2 * cap) + slot
    places = lax.broadcasted_iota(jnp.int32, (tokens, 2 * cap * n_exp), 1)
    pick_low = (places == first).astype(F32).astype(BF16)
    pick_high = (places == first + cap).astype(F32).astype(BF16)
    sent = dot(pick_low, routed_in[:, :halfm], TN) + dot(pick_high, routed_in[:, halfm:], TN)
    outbound[...] = sent.astype(BF16).reshape(outbound.shape)

    def out_copy(k, c):
        rise = 1 - 2 * ((k + c) % 2)
        place = (-k * rise) % chips
        spread = (place + before) % chips
        if spread < chips // 2:
            kind, shift = 0, k % chips
        else:
            kind, shift, spread = 1, (k + away * rise) % chips, spread - chips // 2
        to_ctx = (row - odd + c) * side + col - second + kind
        to_exp = (exp + 2 * turn * shift + 2 * n_exp) % n_exp
        block = spread * 4 + odd * 2 + second
        what = copy_to(
            outbound.at[(2 * chip + 2 * turn * k + 2 * n_exp) % n_exp + c],
            arrived.at[block],
            out_s.at[2 * k + c],
            out_r.at[block],
            ctx=to_ctx,
            exp=to_exp,
        )
        if shift:
            return what, None
        return what, jnp.logical_and(odd == c, second == kind)

    def each_out(act):
        for k in range(chips):
            for c in range(2):
                what, here = out_copy(k, c)
                if here is None:
                    act([what])
                else:

                    @pl.when(jnp.logical_not(here))
                    def _():
                        act([what])

    each_out(start_all)
    arrived[my_block] = outbound[my_expert]

    def g2_copies(j):
        there = (core + 2 * j) * side + col
        return (
            copy_to(
                row_gate, gate_full.at[row], g2_s.at[0, j], g2_r.at[0, row], ctx=there, exp=2 * chip
            ),
            copy_to(
                row_down,
                down_full.at[0, row],
                g2_s.at[1, j],
                g2_r.at[1, row],
                ctx=there,
                exp=2 * chip,
            ),
        )

    def g2_arrivals(src):
        there = src * side + col
        return (
            copy_to(
                row_gate,
                gate_full.at[src],
                g2_s.at[0, 0],
                g2_r.at[0, src],
                ctx=there,
                exp=2 * chip + odd,
            ),
            copy_to(
                row_down,
                down_full.at[0, src],
                g2_s.at[1, 0],
                g2_r.at[1, src],
                ctx=there,
                exp=2 * chip + odd,
            ),
        )

    def u2_copies(kind, j):
        there = row * side + 2 * j + kind
        return (
            copy_to(
                col_up.at[kind],
                up_full.at[:, col],
                u2_s.at[0, kind, j],
                u2_r.at[0, col],
                ctx=there,
                exp=2 * chip + 1,
            ),
            copy_to(
                col_down.at[kind],
                down_full.at[1, :, col],
                u2_s.at[1, kind, j],
                u2_r.at[1, col],
                ctx=there,
                exp=2 * chip + 1,
            ),
        )

    def u2_arrivals(src):
        there = row * side + src
        return (
            copy_to(
                col_up.at[0],
                up_full.at[:, src],
                u2_s.at[0, 0, 0],
                u2_r.at[0, src],
                ctx=there,
                exp=2 * chip + odd,
            ),
            copy_to(
                col_down.at[0],
                down_full.at[1, :, src],
                u2_s.at[1, 0, 0],
                u2_r.at[1, src],
                ctx=there,
                exp=2 * chip + odd,
            ),
        )

    g2_own = jnp.where(jnp.logical_and(core == 0, odd == 0), row // 2, halves)
    u2_own = jnp.where(jnp.logical_and(core == 1, odd == 1), col, side)

    def each_second(act):
        for j in range(halves):

            @pl.when(j != g2_own)
            def _():
                act(g2_copies(j))

        @pl.when(odd == core)
        def _():
            for kind in range(2):
                for j in range(halves):

                    @pl.when(2 * j + kind != u2_own)
                    def _():
                        act(u2_copies(kind, j))

    loop(0, side, unless(col, lambda src: wait_came(g1_arrivals(src))))

    @pl.when(odd == core)
    def _():
        for kind in range(2):
            loop(0, side, unless(row, lambda src: wait_came(u1_arrivals(kind, src))))

    each_second(start_all)

    @pl.when(g2_own < halves)
    def _():
        gate_full[row] = row_gate[...]
        down_full[0, row] = row_down[...]

    @pl.when(u2_own < side)
    def _():
        for r in range(side):
            up_full[r, col] = col_up[second, r]
            down_full[1, r, col] = col_down[second, r]

    def pair_copies(i, which):
        parts = (
            (gate_full.at[i], down_full.at[0, i]),
            (up_full.at[:, i], down_full.at[1, :, i]),
        )[which]
        return [
            copy_to(
                part, part, pair_s.at[2 * which + n, i], pair_r.at[2 * which + n, i], exp=sibling
            )
            for n, part in enumerate(parts)
        ]

    @pl.when(core == 0)
    def _():
        def onward(src):
            @pl.when(jnp.logical_or(src != row, odd == 1))
            def _():
                wait_came(g2_arrivals(src))

            start_all(pair_copies(src, 0))

        loop(0, side, onward)

    @pl.when(core == 1)
    def _():
        def onward(src):
            @pl.when(jnp.logical_or(src != col, odd == 0))
            def _():
                wait_came(u2_arrivals(src))

            start_all(pair_copies(src, 1))

        loop(0, side, onward)

    @pl.when(core == 0)
    def _():
        for i in range(side):
            wait_came(pair_copies(i, 1))

    @pl.when(core == 1)
    def _():
        for i in range(side):
            wait_came(pair_copies(i, 0))

    def out_arrival(block):
        return copy_to(
            outbound.at[0], arrived.at[block], out_s.at[0], out_r.at[block], exp=sibling
        )

    loop(0, n_exp, unless(my_block, lambda block: out_arrival(block).wait_recv()))
    ff = wg_ref.shape[1]
    came = arrived[...].astype(F32)
    rows_in = jnp.concatenate(
        [
            came[:, :cap, :].reshape(n_exp * cap, halfm),
            came[:, cap:, :].reshape(n_exp * cap, halfm),
        ],
        axis=1,
    ).astype(BF16)
    gate_part = dot(rows_in, gate_full[...].reshape(model, ff))
    up_part = dot(rows_in, up_full[...].reshape(model, ff))
    activated = (silu(gate_part) * up_part).astype(BF16)
    blocks = n_ctx // 2
    for j in range(blocks):
        parts = []
        for i in (j, j + blocks):
            down = jnp.concatenate(
                [down_full[0, i // side, i % side], down_full[1, i // side, i % side]], axis=0
            )
            parts.append(dot(activated, down).reshape(n_exp, cap, lanes))
        answer[:, :, j * lanes : (j + 1) * lanes] = jnp.concatenate(parts, axis=1).astype(BF16)

    def back_copy(block):
        far = (block // 4 + chips - reach) * my_up + 2 * chips
        return copy_to(
            answer.at[block],
            returned.at[my_expert],
            back_s.at[block],
            back_r.at[my_expert],
            ctx=beside(block % 4),
            exp=2 * ((chip + far) % chips) + core,
        )

    def back_arrival(expert):
        return copy_to(
            answer.at[0], returned.at[expert], back_s.at[0], back_r.at[expert], exp=sibling
        )

    loop(0, n_exp, unless(my_block, lambda block: back_copy(block).start()))
    returned[my_expert] = answer[my_block]

    halo_copy.wait_send()
    loop(1, chips, lambda d: col_copy(d).wait_send())
    for d in range(1, side):
        wait_sent(band1_copies(d))
        wait_sent(band2_copies(d))
    for d in range(side):
        wait_sent(core_copies(d))
    loop(0, heads, unless(mine, lambda h: ab_copy(h).wait_send()))

    @pl.when(composer)
    def _():
        loop(0, n_ctx, unless(ctx, lambda to: st_copy(to).wait_send()))

    wait_sent(zx_copies)
    each_first(0, wait_sent)
    each_first(1, wait_sent)
    each_second(wait_sent)

    @pl.when(core == 0)
    def _():
        for i in range(side):
            wait_sent(pair_copies(i, 0))

    @pl.when(core == 1)
    def _():
        for i in range(side):
            wait_sent(pair_copies(i, 1))

    each_out(wait_sent)
    loop(0, n_exp, unless(my_block, lambda block: back_copy(block).wait_send()))
    loop(0, n_exp, unless(my_expert, lambda expert: back_arrival(expert).wait_recv()))

    back = returned[...].reshape(2 * cap * n_exp, halfm)
    weight = column(rw_ref[...])
    for pick, at in ((pick_low, slice(0, halfm)), (pick_high, slice(halfm, model))):
        fetched = dot(pick, back)
        out_ref[:, at] = (hidden[:, at].astype(F32) + weight * fetched).astype(BF16)


def on_device(n_ctx, n_exp, *args):
    (qkv, taps, lgate, beta, z, gain, ow, res, post, ids, rw, wg, wu, wd) = args
    tokens, width = qkv.shape[1:]
    heads = lgate.shape[2]
    model = res.shape[2]
    ff = wg.shape[2]
    side = math.isqrt(n_ctx)
    cap = 2 * ids.shape[2] * tokens // n_exp
    inner = heads * HD
    lanes = ow.shape[1]
    chips = n_exp // 2
    sem = pltpu.SemaphoreType.DMA
    operands = (
        qkv[0],
        taps,
        lgate[0].T,
        beta[0].T,
        z[0],
        gain[None],
        ow,
        res[0],
        post[None],
        ids[0].T,
        rw[0].T,
        wg[0],
        wu[0],
        wd[0],
    )
    slots = (n_exp, 2 * cap, model // 2)
    scratch = [pltpu.VMEM(x.shape, x.dtype) for x in operands[:11]]
    scratch += [
        pltpu.VMEM((HALO, width), BF16),
        pltpu.VMEM((8 + tokens, width), F32),
        pltpu.VMEM((heads, tokens, HD), F32),
        pltpu.VMEM((heads, tokens, HD), F32),
        pltpu.VMEM((heads, tokens, tokens), F32),
        pltpu.VMEM((heads, tokens, 2 * HD), BF16),
        pltpu.VMEM((heads, 2 * HD, HD), BF16),
        pltpu.VMEM((n_ctx, 2 * HD, HD), BF16),
        pltpu.VMEM((n_ctx, HD, HD), BF16),
        pltpu.VMEM((heads, HD, HD), BF16),
        pltpu.VMEM((heads, tokens, HD), BF16),
        pltpu.VMEM((heads, tokens, HD), F32),
        pltpu.VMEM((tokens, inner), BF16),
        pltpu.VMEM((chips, ow.shape[0], lanes), BF16),
        pltpu.VMEM((side, side, chips, 2, ow.shape[0], lanes), BF16),
        pltpu.VMEM((tokens, model), BF16),
        pltpu.VMEM((side, side, model // n_ctx, ff), BF16),
        pltpu.VMEM((side, side, model // n_ctx, ff), BF16),
        pltpu.VMEM((2, side, side, ff // 2, lanes), BF16),
        pltpu.VMEM(slots, BF16),
        pltpu.VMEM(slots, BF16),
        pltpu.VMEM(slots, BF16),
        pltpu.VMEM(slots, BF16),
        pltpu.VMEM((model // n_ctx, ff), BF16),
        pltpu.VMEM((model // n_ctx, ff), BF16),
        pltpu.VMEM((ff, lanes), BF16),
        pltpu.VMEM((side, model // n_ctx, ff), BF16),
        pltpu.VMEM((side, ff // 2, lanes), BF16),
        pltpu.VMEM((2, side, model // n_ctx, ff), BF16),
        pltpu.VMEM((2, side, ff // 2, lanes), BF16),
        sem((11,)),
        sem((4,)),
        sem((3,)),
        sem((3,)),
        sem((1,)),
        sem((1,)),
        sem((chips,)),
        sem((chips,)),
        sem((2, side)),
        sem((2, side)),
        sem((2, side)),
        sem((2, side)),
        sem((2, side)),
        sem((2, side)),
        sem((heads,)),
        sem((n_ctx,)),
        sem((n_ctx,)),
        sem((heads,)),
        sem((2, side)),
        sem((2, side)),
        sem((2, 2, side)),
        sem((2, 2, side)),
        sem((2, side)),
        sem((2, side)),
        sem((2, 2, side)),
        sem((2, side)),
        sem((4, side)),
        sem((4, side)),
        sem((n_exp,)),
        sem((n_exp,)),
        sem((n_exp,)),
        sem((n_exp,)),
    ]
    out = pl.pallas_call(
        functools.partial(kernel, n_ctx, n_exp, side),
        out_shape=jax.ShapeDtypeStruct((tokens, model), BF16),
        in_specs=[pl.BlockSpec(memory_space=pltpu.HBM)] * 14,
        out_specs=pl.BlockSpec(memory_space=pltpu.VMEM),
        scratch_shapes=scratch,
        compiler_params=pltpu.CompilerParams(
            collective_id=0, has_side_effects=True, vmem_limit_bytes=63 * 2**20
        ),
    )(*operands)
    return out[None]


def solution(mesh):
    placed = (
        P("exp", "ctx", None),
        P(),
        P("exp", "ctx", None),
        P("exp", "ctx", None),
        P("exp", "ctx", None),
        P(),
        P("exp", "ctx"),
        P("exp", "ctx", None),
        P(),
        P("exp", "ctx", None),
        P("exp", "ctx", None),
        P("exp", "ctx", None),
        P("exp", "ctx", None),
        P("exp", None, "ctx"),
    )
    return jax.shard_map(
        functools.partial(on_device, mesh.shape["ctx"], mesh.shape["exp"]),
        mesh=mesh,
        in_specs=placed,
        out_specs=P("exp", "ctx", None),
        check_vma=False,
    )
```
